128 devices in a mesh: dp: 32 (over y, z, core), fsdp: 4 (over x).
Axes of the slice: x: 4, y: 4, z: 4, core: 2. Of those that a mesh axis runs over, the one named last changes fastest.
Arguments:
- stash: bfloat16 [32, 4, 32, 32, 1024], P('dp', 'fsdp'), may hold values from -6 to 6
- stash_place: int32 [32, 32], replicated, may hold values from 0 to 1023, as said below
- pack_start: int32 [131072], P(('dp', 'fsdp')), may hold values from 0 to 1023, as said below
- d_out: bfloat16 [131072, 1536], P(('dp', 'fsdp')), may hold values from -6 to 6
- out_weight: bfloat16 [768, 1536], P('fsdp'), may hold values from -0.21875 to 0.21875
Outputs:
- grad_query: bfloat16 [131072, 768], P(('dp', 'fsdp'))
- grad_keyval: bfloat16 [131072, 256], P(('dp', 'fsdp'))
- grad_weight: float32 [768, 1536], P('fsdp')
The draws below stay inside these ranges and needn't reach their ends.
Inputs may be any that keep to these rules, and one draw needn't show every extreme that they name: `pack_start`: each value is the index, among its device's 1024 rows, of the first row of the row's pack: packs are runs of consecutive rows of one device, never crossing devices, of at most 1024 rows, and some pack has exactly 1024 rows. `stash_place`: A permutation of 0 to 1023; one placement serves all 4 fsdp shards of a group alike. Exactly 16 blocks of every group are held by other groups, each by a different group; a group holds exactly 1 block of each other group that it holds any of, and blocks of exactly 16 other groups.
All inputs are finite; a program needn't handle non-finite values.
Results may differ from the reference program's by a relative error of at most 0.012.
The reference program's roundings to bfloat16 on the way count: a program that leaves them out, or rounds other values in their place, can miss the bound.
Values may be sent and summed in bfloat16 or wider, within the bound.
No kernel may reach another device: no remote copies, remote signals or barrier semaphores. Data moves between devices by JAX's collectives and lax.ppermute only.
A program may use at most 128 MiB of HBM per device.

```python
import jax
import jax.numpy as jnp
from jax import lax

D = 1536
HQ = 6
HD = 128
QKW = 1024
TOK_DEV = 1024
PACK = 1024
TILE = 256
BLK = 32
NB = 32
EV = 16
TOKENS = 131072
N_DP = 32
N_FSDP = 4


def pack_plan(key):
    level = jax.random.randint(jax.random.fold_in(key, 101), (N_DP,), 0, 5)
    forced = jax.random.randint(jax.random.fold_in(key, 102), (), 0, N_DP)
    level = jnp.where(jnp.arange(N_DP) == forced, 4, level).astype(jnp.int32)
    return (level, forced)


def draw_pack_start(key, part):
    level, forced = pack_plan(key)
    key = jax.random.fold_in(key, 1)
    devices = N_DP * N_FSDP
    count = TOK_DEV // max(1, PACK // 32) + 2
    group_cap = PACK // 16 * 2 ** level
    device_cap = jnp.repeat(group_cap, N_FSDP)
    lowest = device_cap // 2
    raw = jax.random.randint(key, (devices, count), 0, 1 << 20)
    lengths = lowest[:, None] + raw % (device_cap - lowest + 1)[:, None]
    owner_group = jnp.arange(devices) // N_FSDP
    lengths = lengths.at[:, 0].set(jnp.where(owner_group == forced, PACK, lengths[:, 0]))
    bounds = jnp.cumsum(lengths, axis=1).astype(jnp.int32)
    spots = jnp.arange(TOK_DEV, dtype=jnp.int32)
    where_at = jax.vmap(lambda edges: jnp.searchsorted(edges, spots, side='right'))(bounds)
    starts = jnp.concatenate([jnp.zeros((devices, 1), jnp.int32), bounds], axis=1)
    first_rows = jnp.take_along_axis(starts, where_at.astype(jnp.int32), axis=1)
    return first_rows.reshape(-1).astype(jnp.int32)


def draw_stash_place(key, part):
    level, forced = pack_plan(key)
    key = jax.random.fold_in(key, 2)
    shuffled = jax.random.permutation(jax.random.fold_in(key, 1), N_DP).astype(jnp.int32)
    score = level * N_DP + shuffled
    order = jnp.argsort(score).astype(jnp.int32)
    position = jnp.argsort(order).astype(jnp.int32)
    half = N_DP // 2
    noise = jax.random.randint(jax.random.fold_in(key, 2), (N_DP, NB), 0, 1 << 16)
    picked = jnp.argsort(noise * NB + jnp.arange(NB)[None, :], axis=1).astype(jnp.int32)
    evicted = jnp.arange(EV, dtype=jnp.int32)
    heavy = position >= half
    rank = jnp.where(heavy, position - half, position)
    stride = evicted
    partner_rank = jnp.where(heavy[:, None], (rank[:, None] + stride[None, :]) % half, (rank[:, None] - stride[None, :]) % half)
    partner = jnp.where(heavy[:, None], order[partner_rank], order[half + partner_rank])
    partner_slot = picked[partner, jnp.broadcast_to(evicted[None, :], partner.shape)]
    place = jnp.arange(N_DP, dtype=jnp.int32)[:, None] * NB + jnp.arange(NB, dtype=jnp.int32)[None, :]
    group_rows = jnp.broadcast_to(jnp.arange(N_DP, dtype=jnp.int32)[:, None], (N_DP, EV))
    place = place.at[group_rows, picked[:, :EV]].set(partner * NB + partner_slot)
    return place.astype(jnp.int32)


def draw_stash(key, part):
    key = jax.random.fold_in(key, 3)
    shape = (N_DP, N_FSDP, NB, BLK, QKW)
    base = jnp.clip(jax.random.normal(jax.random.fold_in(key, 1), shape, jnp.float32), -6.0, 6.0)
    return base.astype(jnp.bfloat16)


def levels(own_key, dims, cuts, least, top_value):
    gain, own = 1.0, jax.random.fold_in(own_key, 6)
    for dim, parts in cuts:
        heights = jnp.exp(jax.random.uniform(jax.random.fold_in(own, dim), (parts,), jnp.float32, least / len(cuts), top_value / len(cuts)))
        gain = gain * jnp.repeat(heights, dims[dim] // parts).reshape([-1 if axis == dim else 1 for axis in range(len(dims))])
    return gain


def gaussian(own_key, dims, scale, reach, shards=(), kind=jnp.bfloat16):
    drawn = scale * jax.random.normal(own_key, dims, jnp.float32)
    if shards:
        drawn = drawn * levels(own_key, dims, shards, -0.22, 0.18)
    return jnp.clip(drawn, -reach, reach).astype(kind)


def setup_inputs(seed: int = 0) -> dict:
    key_list = jax.random.split(jax.random.key(seed), 6)
    return {
        "stash": draw_stash(jax.random.fold_in(key_list[5], 71), 0),
        "stash_place": draw_stash_place(jax.random.fold_in(key_list[5], 71), 0),
        "pack_start": draw_pack_start(jax.random.fold_in(key_list[5], 71), 0),
        "d_out": gaussian(key_list[3], (TOKENS, D), 1.0, 6.0, ((0, 128),)),
        "out_weight": gaussian(key_list[4], (HQ * HD, D), (HQ * HD) ** -0.5, 0.21875, ((0, 4),)),
    }


def owned_rows(stash, stash_place):
    flat = jnp.transpose(stash, (1, 0, 2, 3, 4)).reshape(N_FSDP, N_DP * NB, BLK, QKW)
    taken = jnp.take(flat, stash_place.reshape(-1).astype(jnp.int32), axis=1)
    taken = taken.reshape(N_FSDP, N_DP, NB * BLK, QKW)
    return jnp.transpose(taken, (1, 0, 2, 3)).reshape(N_DP * N_FSDP, TOK_DEV, QKW)


def device_attention(operands):
    rows, upstream_all, pack = operands
    query_width = HQ * HD
    scale = HD ** -0.5
    span = PACK + TILE
    padded = jnp.concatenate([jnp.zeros((PACK, QKW), rows.dtype), rows], axis=0)
    pad_pack = jnp.concatenate([jnp.full((PACK,), -1, jnp.int32), pack], axis=0)

    def step(buffer, index):
        start = (index * TILE).astype(jnp.int32)
        query_rows = lax.dynamic_slice_in_dim(rows, start, TILE, 0)
        query = query_rows[:, :query_width].reshape(TILE, HQ, HD).astype(jnp.float32)
        window = lax.dynamic_slice_in_dim(padded, start, span, 0)
        keys = window[:, query_width:query_width + HD].astype(jnp.float32)
        values = window[:, query_width + HD:].astype(jnp.float32)
        query_pack = lax.dynamic_slice_in_dim(pack, start, TILE, 0)
        key_pack = lax.dynamic_slice_in_dim(pad_pack, start, span, 0)
        query_index = start + jnp.arange(TILE, dtype=jnp.int32)
        key_index = start - PACK + jnp.arange(span, dtype=jnp.int32)
        allowed = (query_pack[:, None] == key_pack[None, :]) & (key_index[None, :] <= query_index[:, None])
        scores = jnp.einsum("qhd,kd->hqk", query, keys) * scale
        scores = jnp.where(allowed[None], scores, -jnp.inf)
        top = jnp.max(scores, axis=2, keepdims=True)
        expo = jnp.exp(scores - top)
        prob = expo / jnp.sum(expo, axis=2, keepdims=True)
        weights = lax.optimization_barrier(prob.astype(jnp.bfloat16)).astype(jnp.float32)
        attended = jnp.einsum("hqk,kd->qhd", weights, values).astype(jnp.bfloat16)
        attended_wide = lax.optimization_barrier(attended).astype(jnp.float32)
        upstream = lax.dynamic_slice_in_dim(upstream_all, start, TILE, 0).reshape(TILE, HQ, HD).astype(jnp.float32)
        delta = jnp.transpose(jnp.sum(upstream * attended_wide, axis=2))
        grad_prob = jnp.einsum("qhd,kd->hqk", upstream, values)
        dscore = (prob * (grad_prob - delta[:, :, None])).astype(jnp.bfloat16)
        dscore = lax.optimization_barrier(dscore).astype(jnp.float32)
        grad_q = (jnp.einsum("hqk,kd->qhd", dscore, keys) * scale).astype(jnp.bfloat16)
        grad_key = jnp.einsum("hqk,qhd->kd", dscore, query)
        grad_value = jnp.einsum("hqk,qhd->kd", weights, upstream)
        piece = lax.dynamic_slice_in_dim(buffer, start, span, 0) + jnp.concatenate([grad_key, grad_value], axis=1)
        buffer = lax.dynamic_update_slice_in_dim(buffer, piece, start, 0)
        return buffer, (attended.reshape(TILE, query_width), grad_q.reshape(TILE, query_width))

    buffer_start = jnp.zeros((PACK + TOK_DEV, 2 * HD), jnp.float32)
    buffer, (attended, grad_q) = lax.scan(step, buffer_start, jnp.arange(TOK_DEV // TILE, dtype=jnp.int32))
    key_value = buffer[PACK:]
    grad_kv = jnp.concatenate([key_value[:, :HD] * scale, key_value[:, HD:]], axis=1).astype(jnp.bfloat16)
    return attended.reshape(TOK_DEV, query_width), grad_q.reshape(TOK_DEV, query_width), grad_kv


def reference(stash, stash_place, pack_start, d_out, out_weight):
    rows = owned_rows(stash, stash_place)
    d_attn = jnp.dot(d_out, out_weight.T, preferred_element_type=jnp.float32).astype(jnp.bfloat16)
    devices = N_DP * N_FSDP
    attended, grad_q, grad_kv = lax.map(device_attention, (rows, d_attn.reshape(devices, TOK_DEV, HQ * HD), pack_start.reshape(devices, TOK_DEV)))
    attended = attended.reshape(TOKENS, HQ * HD)
    grad_weight = jnp.dot(attended.T, d_out, preferred_element_type=jnp.float32) * (TOKENS ** -0.5)
    return grad_q.reshape(TOKENS, HQ * HD), grad_kv.reshape(TOKENS, 2 * HD), grad_weight
```

```python
import functools

import jax
import jax.numpy as jnp
from jax import lax
from jax.experimental import pallas as pl
from jax.experimental.pallas import tpu as pltpu
from jax.sharding import PartitionSpec as P

HQ = 6
HD = 128
TILE = 256
TOK = 1024
TILES = TOK // TILE
D = 1536
HALF = D // 2
NB = 32
BLK = 32
WIDTH = 1024
N_FSDP = 4
SHARD = HQ * HD // N_FSDP
SCALE = HD ** (-0.5)
EXP2_SCALE = SCALE * 1.4426950408889634
KEY = slice(HQ * HD, (HQ + 1) * HD)
VALUE = slice((HQ + 1) * HD, (HQ + 2) * HD)
HEADS_A = (0, 2, 3, 5)
HEADS_B = (1, 4)
NT = (((1,), (1,)), ((), ()))
NN = (((1,), (0,)), ((), ()))
ANY = pl.BlockSpec(memory_space=pl.ANY)
SMEM = pl.BlockSpec(memory_space=pltpu.SMEM)
VMEM = pl.BlockSpec(memory_space=pltpu.VMEM)
PARAMS = pltpu.CompilerParams(vmem_limit_bytes=56 * 1024 * 1024)
BF16 = jnp.bfloat16
F32 = jnp.float32


def dot(a, b, dims):
    return lax.dot_general(a, b, dims, preferred_element_type=F32)


def shape(dims, dtype=BF16):
    return jax.ShapeDtypeStruct(dims, dtype)


def cost(flops, size, exps=0):
    return pl.CostEstimate(flops=int(flops), bytes_accessed=int(size), transcendentals=int(exps))


def outgoing_kernel(chosen_ref, held_ref, out_ref, sems):
    copies = [
        pltpu.make_async_copy(held_ref.at[chosen_ref[p]], out_ref.at[p], sems.at[p])
        for p in range(NB)
    ]
    for copy in copies:
        copy.start()
    for copy in copies:
        copy.wait()


def pack_outgoing(chosen, held):
    return pl.pallas_call(
        outgoing_kernel,
        out_shape=shape((NB, BLK, WIDTH)),
        in_specs=[SMEM, ANY],
        out_specs=ANY,
        scratch_shapes=[pltpu.SemaphoreType.DMA((NB,))],
        compiler_params=PARAMS,
        name="pack_outgoing",
        cost_estimate=cost(0, 4 * 2**20),
    )(chosen, held)


def d_attn_kernel(x_ref, w0, w1, w2, w3, dout_ref, out_ref):
    x = x_ref[0]
    for k, w in enumerate((w0, w1, w2, w3)):
        shard = lax.rem(x - k + N_FSDP, N_FSDP)
        out_ref[shard] = dot(w[...], dout_ref[...], NT).astype(BF16)


def d_attn_transposed(x, weights, dout):
    return pl.pallas_call(
        d_attn_kernel,
        out_shape=shape((N_FSDP, SHARD, TOK)),
        in_specs=[SMEM] + [VMEM] * 5,
        out_specs=VMEM,
        compiler_params=PARAMS,
        name="d_attn",
        cost_estimate=cost(2 * TOK * D * HQ * HD, 8 * 2**20),
    )(x, *weights, dout).reshape(HQ * HD, TOK)


def keep_mask(tile, start):
    width = (tile + 1) * TILE
    key = lax.broadcasted_iota(jnp.int32, (width, TILE), 0)
    query = tile * TILE + lax.broadcasted_iota(jnp.int32, (width, TILE), 1)
    return (key >= start[:, tile * TILE : width]) & (key <= query)


def transposed(x):
    return x.astype(F32).T.astype(BF16)


def forward_head(rows, value_t, masks, head):
    outs, stats = [], []
    for tile in range(TILES):
        width = (tile + 1) * TILE
        query = rows[tile * TILE : width, head * HD : (head + 1) * HD]
        scores = jnp.where(masks[tile], dot(rows[:width, KEY], query, NT), -jnp.inf)
        top = jnp.max(scores, axis=0, keepdims=True)
        expo = jnp.exp2((scores - top) * EXP2_SCALE)
        total = jnp.sum(expo, axis=0, keepdims=True)
        weights = (expo * (1.0 / total)).astype(BF16)
        outs.append(dot(value_t[:, :width], weights, NN).astype(BF16))
        stats.append(top * EXP2_SCALE + jnp.log2(total))
    return jnp.concatenate(outs, axis=1), jnp.concatenate(stats, axis=1)


def forward_body(heads, core_ref, rows, pack_ref, dout, wait_dout, attn_ref, stat_ref, keep_ref, send_ref, value_t):
    value_t[...] = transposed(rows[:, VALUE])
    start = pack_ref[...]
    masks = [keep_mask(tile, start) for tile in range(TILES)]
    for i, head in enumerate(heads):
        attn, stat = forward_head(rows, value_t, masks, head)
        attn_ref[i * HD : (i + 1) * HD, :] = attn
        stat_ref[i : i + 1, :] = stat
    wait_dout()
    core = core_ref[0]
    mine = pl.multiple_of(core * HALF, HALF)
    other = pl.multiple_of((1 - core) * HALF, HALF)
    send_ref[...] = dot(attn_ref[...], dout[:, pl.ds(other, HALF)], NN).astype(BF16)
    keep_ref[...] = dot(attn_ref[...], dout[:, pl.ds(mine, HALF)], NN).astype(BF16)


def forward_first_kernel(
    heads, core_ref, src_ref, held_ref, inc_ref, pack_ref, dout_hbm,
    attn_ref, stat_ref, keep_ref, send_ref, rows_out, rows, dout, value_t, sems, dout_sem, rows_sem,
):
    for b in range(NB):
        block = rows.at[pl.ds(b * BLK, BLK), :]
        source = src_ref[b]

        @pl.when(source < NB)
        def _(block=block, source=source, b=b):
            pltpu.make_async_copy(held_ref.at[source], block, sems.at[b]).start()

        @pl.when(source >= NB)
        def _(block=block, source=source, b=b):
            pltpu.make_async_copy(inc_ref.at[source - NB], block, sems.at[b]).start()

    dout_copy = pltpu.make_async_copy(dout_hbm, dout, dout_sem)
    dout_copy.start()
    for b in range(NB):
        pltpu.make_async_copy(held_ref.at[0], rows.at[pl.ds(b * BLK, BLK), :], sems.at[b]).wait()
    rows_copy = pltpu.make_async_copy(rows, rows_out, rows_sem)
    rows_copy.start()
    forward_body(
        heads, core_ref, rows, pack_ref, dout, dout_copy.wait, attn_ref, stat_ref, keep_ref, send_ref, value_t
    )
    rows_copy.wait()


def forward_next_kernel(
    heads, core_ref, rows, pack_ref, dout_hbm, attn_ref, stat_ref, keep_ref, send_ref, dout, value_t, dout_sem
):
    dout_copy = pltpu.make_async_copy(dout_hbm, dout, dout_sem)
    dout_copy.start()
    forward_body(
        heads, core_ref, rows, pack_ref, dout, dout_copy.wait, attn_ref, stat_ref, keep_ref, send_ref, value_t
    )


def forward_outs(heads):
    n = len(heads) * HD
    return [shape((n, TOK)), shape((8, TOK), F32), shape((n, HALF)), shape((n, HALF))]


def forward_cost(heads):
    n = len(heads)
    return cost(n * 4 * 10**9, 8 * 2**20, n * 655360)


def forward_first(core, src, held, inc, pack, dout):
    return pl.pallas_call(
        functools.partial(forward_first_kernel, HEADS_A),
        out_shape=forward_outs(HEADS_A) + [shape((TOK, WIDTH))],
        in_specs=[SMEM, SMEM, ANY, ANY, VMEM, ANY],
        out_specs=[VMEM] * 4 + [ANY],
        scratch_shapes=[
            pltpu.VMEM((TOK, WIDTH), BF16),
            pltpu.VMEM((TOK, D), BF16),
            pltpu.VMEM((HD, TOK), BF16),
            pltpu.SemaphoreType.DMA((NB,)),
            pltpu.SemaphoreType.DMA,
            pltpu.SemaphoreType.DMA,
        ],
        compiler_params=PARAMS,
        name="forward_first",
        cost_estimate=forward_cost(HEADS_A),
    )(core, src, held, inc, pack, dout)


def forward_next(core, rows, pack, dout):
    return pl.pallas_call(
        functools.partial(forward_next_kernel, HEADS_B),
        out_shape=forward_outs(HEADS_B),
        in_specs=[SMEM, VMEM, VMEM, ANY],
        out_specs=[VMEM] * 4,
        scratch_shapes=[
            pltpu.VMEM((TOK, D), BF16),
            pltpu.VMEM((HD, TOK), BF16),
            pltpu.SemaphoreType.DMA,
        ],
        compiler_params=PARAMS,
        name="forward_next",
        cost_estimate=forward_cost(HEADS_B),
    )(core, rows, pack, dout)


def backward_kernel(heads, at, first, final, rows, pack_ref, dt_hbm, attn_ref, stat_ref, *rest):
    if first:
        dq_out, kv_ref, key_t, weight_t, score_t, dq, dt, dt_sems, dq_sems = rest
        acc_ref = None
    else:
        acc_ref, _, dq_out, kv_ref, key_t, weight_t, score_t, dq, dt, dt_sems, dq_sems = rest
    loads = [
        pltpu.make_async_copy(dt_hbm.at[pl.ds(h * HD, HD), :], dt.at[i], dt_sems.at[i])
        for i, h in enumerate(heads)
    ]
    for load in loads:
        load.start()
    key_t[...] = transposed(rows[:, KEY])
    start = pack_ref[...]
    masks = [keep_mask(tile, start) for tile in range(TILES)]
    for load in loads:
        load.wait()
    stores = []
    for i, head in enumerate(heads):
        up = dt[i]
        attn = attn_ref[i * HD : (i + 1) * HD, :]
        delta = jnp.sum(up.astype(F32) * attn.astype(F32), axis=0, keepdims=True)
        stat = stat_ref[at + i : at + i + 1, :]
        for tile in range(TILES):
            width = (tile + 1) * TILE
            span = slice(tile * TILE, width)
            spot = slice(i * TOK + tile * TILE, i * TOK + width)
            scores = dot(rows[:width, KEY], rows[span, head * HD : (head + 1) * HD], NT)
            prob = jnp.exp2(jnp.where(masks[tile], scores * EXP2_SCALE - stat[:, span], -jnp.inf))
            weight_t[:width, spot] = prob.astype(BF16)
            dprob = dot(rows[:width, VALUE], up[:, span], NN)
            dscore = (prob * (dprob - delta[:, span])).astype(BF16)
            score_t[:width, spot] = dscore
            dq_t = dot(key_t[:, :width], dscore, NN) * SCALE
            dq[i, span, :] = dq_t.T.astype(BF16)
        store = pltpu.make_async_copy(dq.at[i], dq_out.at[:, pl.ds(head * HD, HD)], dq_sems.at[i])
        store.start()
        stores.append(store)
    for tile in range(TILES):
        span = slice(tile * TILE, (tile + 1) * TILE)
        dk = jnp.zeros((TILE, HD), F32) if first else acc_ref[span, :HD]
        dv = jnp.zeros((TILE, HD), F32) if first else acc_ref[span, HD:]
        for i, head in enumerate(heads):
            spot = slice(i * TOK + tile * TILE, (i + 1) * TOK)
            dk = dk + dot(score_t[span, spot], rows[tile * TILE :, head * HD : (head + 1) * HD], NN)
            dv = dv + dot(weight_t[span, spot], dt[i, :, tile * TILE :], NT)
        if final:
            dk, dv = dk * SCALE, dv
        kv_ref[span, :HD] = dk.astype(kv_ref.dtype)
        kv_ref[span, HD:] = dv.astype(kv_ref.dtype)
    for store in stores:
        store.wait()


def backward(heads, at, final, rows, pack, d_attn_t, attn_t, stats, carry):
    n = len(heads)
    first = carry is None
    args = [rows, pack, d_attn_t, attn_t, stats] + ([] if first else list(carry))
    whole = lambda dims: pl.BlockSpec(dims, lambda i: (0, 0))
    in_specs = [
        whole((TOK, WIDTH)),
        whole((1, TOK)),
        ANY,
        pl.BlockSpec((n * HD, TOK), lambda i: (at // n, 0)),
        whole((8, TOK)),
    ] + ([] if first else [whole((TOK, 2 * HD)), ANY])
    return pl.pallas_call(
        functools.partial(backward_kernel, heads, at, first, final),
        grid=(1,),
        out_shape=[shape((TOK, HQ * HD)), shape((TOK, 2 * HD), BF16 if final else F32)],
        in_specs=in_specs,
        out_specs=[ANY, whole((TOK, 2 * HD))],
        scratch_shapes=[
            pltpu.VMEM((HD, TOK), BF16),
            pltpu.VMEM((TOK, n * TOK), BF16),
            pltpu.VMEM((TOK, n * TOK), BF16),
            pltpu.VMEM((n, TOK, HD), BF16),
            pltpu.VMEM((n, HD, TOK), BF16),
            pltpu.SemaphoreType.DMA((n,)),
            pltpu.SemaphoreType.DMA((n,)),
        ],
        input_output_aliases={} if first else {6: 0},
        compiler_params=PARAMS,
        name="backward",
        cost_estimate=cost(n * 5 * 10**9, 8 * 2**20, n * 655360),
    )(*args)


def add_pair_kernel(x_ref, keep_ref, got_ref, *outs):
    x = x_ref[0]
    for k, out in enumerate(outs):
        shard = lax.rem(x + k, N_FSDP)
        out[...] = (keep_ref[shard].astype(F32) + got_ref[shard].astype(F32)).astype(out.dtype)


def add_pair(x, keep, got):
    rows = keep.shape[0] // N_FSDP
    dims = (rows, HALF)
    return pl.pallas_call(
        add_pair_kernel,
        out_shape=[shape(dims, F32)] + [shape(dims)] * 3,
        in_specs=[SMEM, VMEM, VMEM],
        out_specs=[VMEM] * 4,
        compiler_params=PARAMS,
        name="add_pair",
        cost_estimate=cost(4 * rows * HALF, 10 * rows * HALF * 2),
    )(x, keep.reshape(N_FSDP, *dims), got.reshape(N_FSDP, *dims))


def sum4(parts):
    total = parts[0].astype(F32)
    for part in parts[1:]:
        total = total + part.astype(F32)
    return total


def split_z_kernel(z_ref, *refs):
    a, b, outs, total = refs[:4], refs[4:8], refs[8:12], refs[12]
    rows_a, rows_b = a[0].shape[0], b[0].shape[0]
    total[:rows_a, :] = sum4([r[...] for r in a])
    total[rows_a:, :] = sum4([r[...] for r in b])
    part = (rows_a + rows_b) // 4
    z = z_ref[0]
    for k, out in enumerate(outs):
        at = pl.multiple_of(lax.rem(z + k, 4) * part, part)
        out[...] = total[pl.ds(at, part), :].astype(out.dtype)


def split_z(z, a, b):
    dims = (SHARD // 4, HALF)
    return pl.pallas_call(
        split_z_kernel,
        out_shape=[shape(dims, F32)] + [shape(dims)] * 3,
        in_specs=[SMEM] + [VMEM] * 8,
        out_specs=[VMEM] * 4,
        scratch_shapes=[pltpu.VMEM((SHARD, HALF), F32)],
        compiler_params=PARAMS,
        name="split_z",
        cost_estimate=cost(4 * SHARD * HALF, 10 * SHARD * HALF),
    )(z, *a, *b)


def sum4_kernel(factor, *refs):
    refs[4][...] = (sum4([r[...] for r in refs[:4]]) * factor).astype(BF16)


def sum_four(parts, factor=1.0):
    return pl.pallas_call(
        functools.partial(sum4_kernel, factor),
        out_shape=shape(parts[0].shape),
        in_specs=[VMEM] * 4,
        out_specs=VMEM,
        compiler_params=PARAMS,
        name="sum_four",
        cost_estimate=cost(4 * parts[0].size, 10 * parts[0].size),
    )(*parts)


def lay_out_kernel(pos_ref, *refs):
    own, got, out, half = refs[:4], refs[4:8], refs[8], refs[9]
    x, z, core = pos_ref[0], pos_ref[1], pos_ref[2]
    part = SHARD // 4
    short = len(HEADS_B) * HD // N_FSDP
    for parts, side in ((own, core), (got, 1 - core)):
        for k, ref in enumerate(parts):
            at = pl.multiple_of(lax.rem(z - k + 4, 4) * part, part)
            half[pl.ds(at, part), :] = ref[...].astype(F32)
        columns = pl.ds(pl.multiple_of(side * HALF, HALF), HALF)
        odd = lax.rem(x, 2)

        @pl.when(odd == 0)
        def _(columns=columns):
            out[:, columns] = half[...]

        @pl.when(odd == 1)
        def _(columns=columns):
            out[:short, columns] = half[SHARD - short :, :]
            out[short:, columns] = half[: SHARD - short, :]


def lay_out(pos, own, got):
    return pl.pallas_call(
        lay_out_kernel,
        out_shape=shape((SHARD, D), F32),
        in_specs=[SMEM] + [VMEM] * 8,
        out_specs=VMEM,
        scratch_shapes=[pltpu.VMEM((SHARD, HALF), F32)],
        compiler_params=PARAMS,
        name="lay_out",
        cost_estimate=cost(SHARD * D, 8 * SHARD * D),
    )(pos, *own, *got)


def dp_shift(dy, dz, dc):
    pairs = []
    for i in range(32):
        y, z, c = i // 8, (i // 2) % 4, i % 2
        pairs.append((i, ((y + dy) % 4) * 8 + ((z + dz) % 4) * 2 + (c + dc) % 2))
    return pairs


def x_shift(k):
    return [(i, (i + k) % N_FSDP) for i in range(N_FSDP)]


def per_device(stash, stash_place, pack_start, d_out, out_weight):
    group = lax.axis_index("dp")
    x = lax.axis_index("fsdp")
    core = lax.rem(group, 2)
    z = lax.rem(group // 2, 4)
    held = stash.reshape(NB, BLK, WIDTH)
    peers = jnp.arange(NB, dtype=jnp.int32)
    holder = stash_place // NB
    slot = stash_place % NB
    chosen = jnp.sum(jnp.where((holder == group) & (peers[:, None] != group), slot, 0), axis=1)
    mine = lax.dynamic_index_in_dim(stash_place, group, 0, keepdims=False)
    source = jnp.where(mine // NB == group, mine % NB, NB + mine // NB)
    x1, z1, core1 = x.reshape(1), z.reshape(1), core.reshape(1)

    outgoing = pack_outgoing(jnp.minimum(chosen, NB - 1), held)
    incoming = lax.all_to_all(outgoing, "dp", split_axis=0, concat_axis=0, tiled=True)
    weights = [out_weight] + [lax.ppermute(out_weight, "fsdp", x_shift(k)) for k in (1, 2, 3)]
    d_attn_t = d_attn_transposed(x1, weights, d_out)

    pack = pack_start.reshape(1, TOK)
    swap = dp_shift(0, 0, 1)
    attn_a, stat_a, keep_a, send_a, rows = forward_first(core1, source, held, incoming, pack, d_out)
    got_a = lax.ppermute(send_a, "dp", swap)
    attn_b, stat_b, keep_b, send_b = forward_next(core1, rows, pack, d_out)
    got_b = lax.ppermute(send_b, "dp", swap)

    def over_x(keep, got):
        parts = add_pair(x1, keep, got)
        return [parts[0]] + [lax.ppermute(parts[k], "fsdp", x_shift(k)) for k in (1, 2, 3)]

    parts_a = over_x(keep_a, got_a)
    parts_b = over_x(keep_b, got_b)

    carry = backward(HEADS_A[:2], 0, False, rows, pack, d_attn_t, attn_a, stat_a, None)
    carry = backward(HEADS_A[2:], 2, False, rows, pack, d_attn_t, attn_a, stat_a, carry[::-1])
    grad_query, grad_keyval = backward(HEADS_B, 0, True, rows, pack, d_attn_t, attn_b, stat_b, carry[::-1])

    by_z = split_z(z1, parts_a, parts_b)
    by_z = [by_z[0]] + [lax.ppermute(by_z[k], "dp", dp_shift(0, k, 0)) for k in (1, 2, 3)]
    z_sum = sum_four(by_z)
    by_y = [z_sum] + [lax.ppermute(z_sum, "dp", dp_shift(k, 0, 0)) for k in (1, 2, 3)]
    factor = (TOK * lax.axis_size("dp") * lax.axis_size("fsdp")) ** (-0.5)
    total = sum_four(by_y, factor)
    own = [total] + [lax.ppermute(total, "dp", dp_shift(0, k, 0)) for k in (1, 2, 3)]
    got = [lax.ppermute(part, "dp", swap) for part in own]
    grad_weight = lay_out(jnp.stack([x, z, core]), own, got)
    return (grad_query, grad_keyval, grad_weight)


def solution(mesh):
    in_specs = (
        P("dp", "fsdp", None, None, None),
        P(),
        P(("dp", "fsdp")),
        P(("dp", "fsdp"), None),
        P("fsdp", None),
    )
    out_specs = (P(("dp", "fsdp"), None), P(("dp", "fsdp"), None), P("fsdp", None))
    return jax.shard_map(
        per_device, mesh=mesh, in_specs=in_specs, out_specs=out_specs, check_vma=False
    )
```

```python
import functools

import jax
import jax.numpy as jnp
from jax import lax
from jax.experimental import pallas as pl
from jax.experimental.pallas import tpu as pltpu
from jax.sharding import PartitionSpec as P

HQ = 6
HD = 128
TILE = 256
TOK = 1024
TILES = TOK // TILE
D = 1536
HALF = D // 2
NB = 32
BLK = 32
WIDTH = 1024
N_FSDP = 4
SHARD = HQ * HD // N_FSDP
SCALE = HD ** (-0.5)
EXP2_SCALE = SCALE * 1.4426950408889634
KEY = slice(HQ * HD, (HQ + 1) * HD)
VALUE = slice((HQ + 1) * HD, (HQ + 2) * HD)
NT = (((1,), (1,)), ((), ()))
NN = (((1,), (0,)), ((), ()))
ANY = pl.BlockSpec(memory_space=pl.ANY)
SMEM = pl.BlockSpec(memory_space=pltpu.SMEM)
VMEM = pl.BlockSpec(memory_space=pltpu.VMEM)
HBM = pl.BlockSpec(memory_space=pltpu.HBM)


def params(mib):
    return pltpu.CompilerParams(vmem_limit_bytes=mib * 2**20)


BF16 = jnp.bfloat16
LARGE = 56
F32 = jnp.float32


def dot(a, b, dims):
    return lax.dot_general(a, b, dims, preferred_element_type=F32)


def shape(dims, dtype=BF16):
    return jax.ShapeDtypeStruct(dims, dtype)


def cost(flops, size, exps=0):
    return pl.CostEstimate(flops=int(flops), bytes_accessed=int(size), transcendentals=int(exps))


def d_attn_kernel(x_ref, w0, w1, w2, w3, dout_ref, out_ref, weight, sems):
    @pl.when(pl.program_id(0) == 0)
    def _():
        copies = []
        for k, w in enumerate((w0, w1, w2, w3)):
            at = pl.multiple_of(lax.rem(x_ref[0] - k + N_FSDP, N_FSDP) * SHARD, SHARD)
            copies.append(pltpu.make_async_copy(w, weight.at[pl.ds(at, SHARD), :], sems.at[k]))
        for copy in copies:
            copy.start()
        for copy in copies:
            copy.wait()

    out_ref[...] = dot(weight[...], dout_ref[...], NT).astype(BF16)


def d_attn_transposed(x, weights, dout):
    return pl.pallas_call(
        d_attn_kernel,
        grid=(TILES,),
        out_shape=shape((HQ * HD, TOK)),
        in_specs=[SMEM] + [ANY] * 4 + [pl.BlockSpec((TILE, D), lambda i: (i, 0))],
        out_specs=pl.BlockSpec((HQ * HD, TILE), lambda i: (0, i)),
        scratch_shapes=[pltpu.VMEM((HQ * HD, D), BF16), pltpu.SemaphoreType.DMA((N_FSDP,))],
        compiler_params=params(LARGE),
        name="d_attn",
        cost_estimate=cost(2 * TOK * D * HQ * HD, 8 * 2**20),
    )(x, *weights, dout)


def keep_mask(tile, start):
    width = (tile + 1) * TILE
    key = lax.broadcasted_iota(jnp.int32, (width, TILE), 0)
    query = tile * TILE + lax.broadcasted_iota(jnp.int32, (width, TILE), 1)
    return (key >= start[:, tile * TILE : width]) & (key <= query)


def transposed(x):
    return x.astype(F32).T.astype(BF16)


def forward_tile(rows, value_t, mask, head, tile):
    width = (tile + 1) * TILE
    query = rows[tile * TILE : width, head * HD : (head + 1) * HD]
    scores = jnp.where(mask, dot(rows[:width, KEY], query, NT), -jnp.inf)
    top = jnp.max(scores, axis=0, keepdims=True)
    expo = jnp.exp2((scores - top) * EXP2_SCALE)
    total = jnp.sum(expo, axis=0, keepdims=True)
    weights = (expo * (1.0 / total)).astype(BF16)
    attn = dot(value_t[:, :width], weights, NN).astype(BF16)
    return attn, top * EXP2_SCALE + jnp.log2(total)


def gather_rows(src_ref, held_ref, inc_ref, rows, sems):
    def copy(ref, b, source):
        return pltpu.make_async_copy(ref.at[source], rows.at[pl.ds(b * BLK, BLK), :], sems.at[b])

    for b in range(NB):
        source = src_ref[b]

        @pl.when(source < NB)
        def _(b=b, source=source):
            copy(held_ref, b, source).start()

        @pl.when(source >= NB)
        def _(b=b, source=source):
            copy(inc_ref, b, source - NB).start()

    def wait_rows(tile):
        per_tile = TILE // BLK
        for b in range(tile * per_tile, (tile + 1) * per_tile):
            copy(held_ref, b, 0).wait()

    return wait_rows


def forward_kernel(
    core_ref, src_ref, held_ref, inc_ref, pack_ref, dout_hbm, _w1, _w2, _w3,
    rows_out, attn_out, stat_ref, keep_out, send_out,
    rows, attn_ref, keep_ref, send_ref, dout, value_t, sems, side_sems,
):
    wait_rows = gather_rows(src_ref, held_ref, inc_ref, rows, sems)
    dout_copy = pltpu.make_async_copy(dout_hbm, dout, side_sems.at[0])
    dout_copy.start()
    start = pack_ref[...]
    for tile in range(TILES):
        span = slice(tile * TILE, (tile + 1) * TILE)
        wait_rows(tile)
        value_t[:, span] = transposed(rows[span, VALUE])
        mask = keep_mask(tile, start)
        for head in range(HQ):
            attn, stat = forward_tile(rows, value_t, mask, head, tile)
            attn_ref[head * HD : (head + 1) * HD, span] = attn
            stat_ref[head : head + 1, span] = stat
    rows_copy = pltpu.make_async_copy(rows, rows_out, side_sems.at[1])
    rows_copy.start()
    attn_copy = pltpu.make_async_copy(attn_ref, attn_out, side_sems.at[2])
    attn_copy.start()
    dout_copy.wait()
    core = core_ref[0]
    mine = pl.multiple_of(core * HALF, HALF)
    other = pl.multiple_of((1 - core) * HALF, HALF)
    send_ref[...] = dot(attn_ref[...], dout[:, pl.ds(other, HALF)], NN).astype(BF16)
    send_copy = pltpu.make_async_copy(send_ref, send_out, side_sems.at[3])
    send_copy.start()
    keep_ref[...] = dot(attn_ref[...], dout[:, pl.ds(mine, HALF)], NN).astype(BF16)
    keep_copy = pltpu.make_async_copy(keep_ref, keep_out, side_sems.at[4])
    keep_copy.start()
    for copy in (rows_copy, attn_copy, send_copy, keep_copy):
        copy.wait()


def forward(core, src, held, inc, pack, dout, after):
    n = HQ * HD
    return pl.pallas_call(
        forward_kernel,
        out_shape=[
            shape((TOK, WIDTH)), shape((n, TOK)), shape((8, TOK), F32), shape((n, HALF)), shape((n, HALF))
        ],
        in_specs=[SMEM, SMEM, ANY, ANY, VMEM, ANY] + [ANY] * 3,
        out_specs=[ANY, ANY, VMEM, ANY, ANY],
        scratch_shapes=[
            pltpu.VMEM((TOK, WIDTH), BF16),
            pltpu.VMEM((n, TOK), BF16),
            pltpu.VMEM((n, HALF), BF16),
            pltpu.VMEM((n, HALF), BF16),
            pltpu.VMEM((TOK, D), BF16),
            pltpu.VMEM((HD, TOK), BF16),
            pltpu.SemaphoreType.DMA((NB,)),
            pltpu.SemaphoreType.DMA((5,)),
        ],
        compiler_params=params(LARGE),
        name="forward",
        cost_estimate=cost(12 * 10**9, 8 * 2**20, HQ * 655360),
    )(core, src, held, inc, pack, dout, *after)


PAIR = 2


def backward_kernel(
    rows_hbm, pack_ref, dt_hbm, attn_hbm, stat_ref, _, dq_out, kv_ref,
    rows, dt, attn_ref, key_t, weight_t, score_t, acc, dq, dq_sems, load_sems,
):
    loads = [
        pltpu.make_async_copy(source, target, load_sems.at[i])
        for i, (source, target) in enumerate(((rows_hbm, rows), (dt_hbm, dt), (attn_hbm, attn_ref)))
    ]
    for load in loads:
        load.start()
    for load in loads:
        load.wait()
    key_t[...] = transposed(rows[:, KEY])
    start = pack_ref[...]
    stores = []
    for first in range(0, HQ, PAIR):
        for head in range(first, first + PAIR):
            here = slice(head * HD, (head + 1) * HD)
            up = dt[here, :]
            delta = jnp.sum(up.astype(F32) * attn_ref[here, :].astype(F32), axis=0, keepdims=True)
            stat = stat_ref[head : head + 1, :]
            for tile in range(TILES):
                width = (tile + 1) * TILE
                span = slice(tile * TILE, width)
                at = (head - first) * TOK
                spot = slice(at + tile * TILE, at + width)
                scores = dot(rows[:width, KEY], rows[span, here], NT)
                mask = keep_mask(tile, start)
                prob = jnp.exp2(jnp.where(mask, scores * EXP2_SCALE - stat[:, span], -jnp.inf))
                weight_t[:width, spot] = prob.astype(BF16)
                dprob = dot(rows[:width, VALUE], up[:, span], NN)
                dscore = (prob * (dprob - delta[:, span])).astype(BF16)
                score_t[:width, spot] = dscore
                dq_t = dot(key_t[:, :width], dscore, NN) * SCALE
                dq[head, span, :] = dq_t.T.astype(BF16)
            store = pltpu.make_async_copy(dq.at[head], dq_out.at[:, pl.ds(head * HD, HD)], dq_sems.at[head])
            store.start()
            stores.append(store)
        for tile in range(TILES):
            span = slice(tile * TILE, (tile + 1) * TILE)
            dk = jnp.zeros((TILE, HD), F32) if first == 0 else acc[span, :HD]
            dv = jnp.zeros((TILE, HD), F32) if first == 0 else acc[span, HD:]
            for head in range(first, first + PAIR):
                here = slice(head * HD, (head + 1) * HD)
                at = (head - first) * TOK
                spot = slice(at + tile * TILE, at + TOK)
                dk = dk + dot(score_t[span, spot], rows[tile * TILE :, here], NN)
                dv = dv + dot(weight_t[span, spot], dt[here, tile * TILE :], NT)
            if first + PAIR == HQ:
                kv_ref[span, :HD] = (dk * SCALE).astype(BF16)
                kv_ref[span, HD:] = dv.astype(BF16)
            else:
                acc[span, :HD] = dk
                acc[span, HD:] = dv
    for store in stores:
        store.wait()


def backward(rows, pack, d_attn_t, attn_t, stats, after):
    return pl.pallas_call(
        backward_kernel,
        out_shape=[shape((TOK, HQ * HD)), shape((TOK, 2 * HD))],
        in_specs=[ANY, VMEM, ANY, ANY, VMEM, ANY],
        out_specs=[ANY, VMEM],
        scratch_shapes=[
            pltpu.VMEM((TOK, WIDTH), BF16),
            pltpu.VMEM((HQ * HD, TOK), BF16),
            pltpu.VMEM((HQ * HD, TOK), BF16),
            pltpu.VMEM((HD, TOK), BF16),
            pltpu.VMEM((TOK, PAIR * TOK), BF16),
            pltpu.VMEM((TOK, PAIR * TOK), BF16),
            pltpu.VMEM((TOK, 2 * HD), F32),
            pltpu.VMEM((HQ, TOK, HD), BF16),
            pltpu.SemaphoreType.DMA((HQ,)),
            pltpu.SemaphoreType.DMA((3,)),
        ],
        compiler_params=params(LARGE),
        name="backward",
        cost_estimate=cost(30 * 10**9, 8 * 2**20, HQ * 655360),
    )(rows, pack, d_attn_t, attn_t, stats, after)


def add_pair_kernel(x_ref, keep_ref, got_ref, *outs):
    x = x_ref[0]
    for k, out in enumerate(outs):
        shard = lax.rem(x + k, N_FSDP)
        out[...] = (keep_ref[shard].astype(F32) + got_ref[shard].astype(F32)).astype(out.dtype)


def add_pair(x, keep, got):
    rows = keep.shape[0] // N_FSDP
    dims = (rows, HALF)
    return pl.pallas_call(
        add_pair_kernel,
        out_shape=[shape(dims, F32)] + [shape(dims)] * 3,
        in_specs=[SMEM, VMEM, VMEM],
        out_specs=[VMEM] * 4,
        compiler_params=params(4),
        name="add_pair",
        cost_estimate=cost(4 * rows * HALF, 10 * rows * HALF * 2),
    )(x, keep.reshape(N_FSDP, *dims), got.reshape(N_FSDP, *dims))


def sum4(parts):
    total = parts[0].astype(F32)
    for part in parts[1:]:
        total = total + part.astype(F32)
    return total


def split_z_kernel(z_ref, _, *refs):
    parts, outs, total = refs[:4], refs[4:8], refs[8]
    total[...] = sum4([r[...] for r in parts])
    size = SHARD // 4
    z = z_ref[0]
    for k, out in enumerate(outs):
        at = pl.multiple_of(lax.rem(z + k, 4) * size, size)
        out[...] = total[pl.ds(at, size), :].astype(out.dtype)


def split_z(z, after, parts):
    dims = (SHARD // 4, HALF)
    return pl.pallas_call(
        split_z_kernel,
        out_shape=[shape(dims, F32)] + [shape(dims)] * 3,
        in_specs=[SMEM, ANY] + [VMEM] * 4,
        out_specs=[VMEM] * 4,
        scratch_shapes=[pltpu.VMEM((SHARD, HALF), F32)],
        compiler_params=params(4),
        name="split_z",
        cost_estimate=cost(4 * SHARD * HALF, 10 * SHARD * HALF),
    )(z, after, *parts)


def sum4_kernel(factor, *refs):
    refs[4][...] = (sum4([r[...] for r in refs[:4]]) * factor).astype(BF16)


def sum_four(parts, factor=1.0):
    return pl.pallas_call(
        functools.partial(sum4_kernel, factor),
        out_shape=shape(parts[0].shape),
        in_specs=[VMEM] * 4,
        out_specs=VMEM,
        compiler_params=params(8),
        name="sum_four",
        cost_estimate=cost(4 * parts[0].size, 10 * parts[0].size),
    )(*parts)


def lay_out_kernel(pos_ref, *refs):
    own, got, out = refs[:4], refs[4:8], refs[8]
    z, core = pos_ref[0], pos_ref[1]
    size = SHARD // 4
    for parts, side in ((own, core), (got, 1 - core)):
        columns = pl.ds(pl.multiple_of(side * HALF, HALF), HALF)
        for k, ref in enumerate(parts):
            at = pl.multiple_of(lax.rem(z - k + 4, 4) * size, size)
            out[pl.ds(at, size), columns] = ref[...].astype(F32)


def lay_out(pos, own, got):
    return pl.pallas_call(
        lay_out_kernel,
        out_shape=shape((SHARD, D), F32),
        in_specs=[SMEM] + [VMEM] * 8,
        out_specs=VMEM,
        compiler_params=params(8),
        name="lay_out",
        cost_estimate=cost(SHARD * D, 8 * SHARD * D),
    )(pos, *own, *got)


def dp_shift(dy, dz, dc):
    pairs = []
    for i in range(32):
        y, z, c = i // 8, (i // 2) % 4, i % 2
        pairs.append((i, ((y + dy) % 4) * 8 + ((z + dz) % 4) * 2 + (c + dc) % 2))
    return pairs


def x_shift(k):
    return [(i, (i + k) % N_FSDP) for i in range(N_FSDP)]


def per_device(stash, stash_place, pack_start, d_out, out_weight):
    group = lax.axis_index("dp")
    x = lax.axis_index("fsdp")
    core = lax.rem(group, 2)
    z = lax.rem(group // 2, 4)
    held = stash.reshape(NB, BLK, WIDTH)
    peers = jnp.arange(NB, dtype=jnp.int32)
    holder = stash_place // NB
    slot = stash_place % NB
    chosen = jnp.sum(jnp.where((holder == group) & (peers[:, None] != group), slot, 0), axis=1)
    mine = lax.dynamic_index_in_dim(stash_place, group, 0, keepdims=False)
    source = jnp.where(mine // NB == group, mine % NB, NB + mine // NB)
    x1, z1, core1 = x.reshape(1), z.reshape(1), core.reshape(1)

    incoming = lax.all_to_all(held[chosen], "dp", split_axis=0, concat_axis=0, tiled=True)
    weights = [out_weight] + [lax.ppermute(out_weight, "fsdp", x_shift(k)) for k in (1, 2, 3)]

    pack = pack_start.reshape(1, TOK)
    swap = dp_shift(0, 0, 1)
    rows, attn_t, stats, keep, send = forward(core1, source, held, incoming, pack, d_out, weights[1:])
    d_attn_t = d_attn_transposed(x1, weights, d_out)
    parts = add_pair(x1, keep, lax.ppermute(send, "dp", swap))
    by_x = [parts[0]] + [lax.ppermute(parts[k], "fsdp", x_shift(k)) for k in (1, 2, 3)]
    grad_query, grad_keyval = backward(rows, pack, d_attn_t, attn_t, stats, parts[0])
    by_z = split_z(z1, grad_keyval, by_x)
    by_z = [by_z[0]] + [lax.ppermute(by_z[k], "dp", dp_shift(0, k, 0)) for k in (1, 2, 3)]
    z_sum = sum_four(by_z)
    by_y = [z_sum] + [lax.ppermute(z_sum, "dp", dp_shift(k, 0, 0)) for k in (1, 2, 3)]
    factor = (TOK * lax.axis_size("dp") * lax.axis_size("fsdp")) ** (-0.5)
    total = sum_four(by_y, factor)
    own = [total] + [lax.ppermute(total, "dp", dp_shift(0, k, 0)) for k in (1, 2, 3)]
    got = [lax.ppermute(part, "dp", swap) for part in own]
    grad_weight = lay_out(jnp.stack([z, core]), own, got)
    return (grad_query, grad_keyval, grad_weight)


def solution(mesh):
    in_specs = (
        P("dp", "fsdp", None, None, None),
        P(),
        P(("dp", "fsdp")),
        P(("dp", "fsdp"), None),
        P("fsdp", None),
    )
    out_specs = (P(("dp", "fsdp"), None), P(("dp", "fsdp"), None), P("fsdp", None))
    return jax.shard_map(
        per_device, mesh=mesh, in_specs=in_specs, out_specs=out_specs, check_vma=False
    )
```

```python
import functools

import jax
import jax.numpy as jnp
from jax import lax
from jax.experimental import pallas as pl
from jax.experimental.pallas import tpu as pltpu
from jax.sharding import PartitionSpec as P

HQ = 6
HD = 128
TILE = 256
TOK = 1024
TILES = TOK // TILE
D = 1536
HALF = D // 2
NB = 32
BLK = 32
WIDTH = 1024
N_FSDP = 4
SHARD = HQ * HD // N_FSDP
SCALE = HD ** (-0.5)
EXP2_SCALE = SCALE * 1.4426950408889634
KEY = slice(HQ * HD, (HQ + 1) * HD)
VALUE = slice((HQ + 1) * HD, (HQ + 2) * HD)
NT = (((1,), (1,)), ((), ()))
NN = (((1,), (0,)), ((), ()))
ANY = pl.BlockSpec(memory_space=pl.ANY)
SMEM = pl.BlockSpec(memory_space=pltpu.SMEM)
VMEM = pl.BlockSpec(memory_space=pltpu.VMEM)
HBM = pl.BlockSpec(memory_space=pltpu.HBM)


def params(mib):
    return pltpu.CompilerParams(vmem_limit_bytes=mib * 2**20)


BF16 = jnp.bfloat16
LARGE = 56
F32 = jnp.float32


def dot(a, b, dims):
    return lax.dot_general(a, b, dims, preferred_element_type=F32)


def shape(dims, dtype=BF16):
    return jax.ShapeDtypeStruct(dims, dtype)


TOKEN = shape((8, 128), F32)


def cost(flops, size, exps=0):
    return pl.CostEstimate(flops=int(flops), bytes_accessed=int(size), transcendentals=int(exps))


def d_attn_kernel(pos_ref, *refs):
    own, mine, others, dout_hbm, out_ref, weight, dout, sems, dout_sem = (
        refs[0], refs[1:4], refs[4:7], *refs[7:]
    )
    x, core = pos_ref[0], pos_ref[1]

    def shard_rows(k):
        return pl.ds(pl.multiple_of(lax.rem(x - k + N_FSDP, N_FSDP) * SHARD, SHARD), SHARD)

    loads = [pltpu.make_async_copy(own, weight.at[shard_rows(0), :], sems.at[0])]
    for k in range(1, N_FSDP):
        for i, (part, side) in enumerate(((mine[k - 1], core), (others[k - 1], 1 - core))):
            columns = pl.ds(pl.multiple_of(side * HALF, HALF), HALF)
            loads.append(pltpu.make_async_copy(part, weight.at[shard_rows(k), columns], sems.at[2 * k - 1 + i]))
    block = pltpu.make_async_copy(dout_hbm, dout, dout_sem)
    for load in loads + [block]:
        load.start()
    for load in loads:
        load.wait()
    block.wait()
    out_ref[...] = dot(weight[...], dout[...], NT).astype(BF16)


def d_attn_transposed(pos, own, mine, others, dout):
    return pl.pallas_call(
        d_attn_kernel,
        out_shape=shape((HQ * HD, TOK)),
        in_specs=[SMEM] + [ANY] * 8,
        out_specs=VMEM,
        scratch_shapes=[
            pltpu.VMEM((HQ * HD, D), BF16),
            pltpu.VMEM((TOK, D), BF16),
            pltpu.SemaphoreType.DMA((7,)),
            pltpu.SemaphoreType.DMA,
        ],
        compiler_params=params(LARGE),
        name="d_attn",
        cost_estimate=cost(2 * TOK * D * HQ * HD, 8 * 2**20),
    )(pos, own, *mine, *others, dout)


def keep_mask(tile, start):
    width = (tile + 1) * TILE
    key = lax.broadcasted_iota(jnp.int32, (width, TILE), 0)
    query = tile * TILE + lax.broadcasted_iota(jnp.int32, (width, TILE), 1)
    return (key >= start[:, tile * TILE : width]) & (key <= query)


def transposed(x):
    return x.astype(F32).T.astype(BF16)


def gather_rows(src_ref, held_ref, inc_ref, rows, sems):
    def copy(ref, b, source):
        return pltpu.make_async_copy(ref.at[source], rows.at[pl.ds(b * BLK, BLK), :], sems.at[b])

    for b in range(NB):
        source = src_ref[b]

        @pl.when(source < NB)
        def _(b=b, source=source):
            copy(held_ref, b, source).start()

        @pl.when(source >= NB)
        def _(b=b, source=source):
            copy(inc_ref, b, source - NB).start()

    def wait_rows(tile):
        per_tile = TILE // BLK
        for b in range(tile * per_tile, (tile + 1) * per_tile):
            copy(held_ref, b, 0).wait()

    return wait_rows


def forward_kernel(
    core_ref, src_ref, held_ref, inc_ref, pack_ref, dout_hbm, _,
    rows_out, attn_out, stat_ref, send_out,
    rows, attn_ref, send_ref, dout, value_t, sems, side_sems, attn_sems,
):
    wait_rows = gather_rows(src_ref, held_ref, inc_ref, rows, sems)
    other = pl.ds(pl.multiple_of((1 - core_ref[0]) * HALF, HALF), HALF)
    dout_copy = pltpu.make_async_copy(dout_hbm.at[:, other], dout, side_sems.at[0])
    dout_copy.start()
    rows_copy = pltpu.make_async_copy(rows, rows_out, side_sems.at[1])
    send_copy = pltpu.make_async_copy(send_ref, send_out, side_sems.at[2])
    attn_copies = [
        pltpu.make_async_copy(
            attn_ref.at[pl.ds(h * HD, HD), :], attn_out.at[pl.ds(h * HD, HD), :], attn_sems.at[h]
        )
        for h in range(HQ)
    ]
    start = pack_ref[...]
    for tile in range(TILES):
        width = (tile + 1) * TILE
        span = slice(tile * TILE, width)
        wait_rows(tile)
        if tile == TILES - 1:
            rows_copy.start()
        value_t[:, span] = transposed(rows[span, VALUE])
        mask = keep_mask(tile, start)

        def raw_scores(head, width=width, span=span):
            return dot(rows[:width, KEY], rows[span, head * HD : (head + 1) * HD], NT)

        ahead = raw_scores(0)
        for head in range(HQ):
            here = slice(head * HD, (head + 1) * HD)
            scores = ahead
            if head + 1 < HQ:
                ahead = raw_scores(head + 1)
            scores = jnp.where(mask, scores, -jnp.inf)
            top = jnp.max(scores, axis=0, keepdims=True)
            expo = jnp.exp2((scores - top) * EXP2_SCALE)
            total = jnp.sum(expo, axis=0, keepdims=True)
            weights = (expo * (1.0 / total)).astype(BF16)
            attn_ref[here, span] = dot(value_t[:, :width], weights, NN).astype(BF16)
            stat_ref[head : head + 1, span] = top * EXP2_SCALE + jnp.log2(total)
    for copy in attn_copies:
        copy.start()
    dout_copy.wait()
    send_ref[...] = dot(attn_ref[...], dout[...], NN).astype(BF16)
    send_copy.start()
    for copy in (rows_copy, *attn_copies, send_copy):
        copy.wait()


def forward(core, src, held, inc, pack, dout, after):
    n = HQ * HD
    return pl.pallas_call(
        forward_kernel,
        out_shape=[
            shape((TOK, WIDTH)), shape((n, TOK)), shape((8, TOK), F32), shape((n, HALF))
        ],
        in_specs=[SMEM, SMEM, ANY, ANY, VMEM, ANY, ANY],
        out_specs=[ANY, ANY, VMEM, ANY],
        scratch_shapes=[
            pltpu.VMEM((TOK, WIDTH), BF16),
            pltpu.VMEM((n, TOK), BF16),
            pltpu.VMEM((n, HALF), BF16),
            pltpu.VMEM((TOK, HALF), BF16),
            pltpu.VMEM((HD, TOK), BF16),
            pltpu.SemaphoreType.DMA((NB,)),
            pltpu.SemaphoreType.DMA((3,)),
            pltpu.SemaphoreType.DMA((HQ,)),
        ],
        compiler_params=params(LARGE),
        name="forward",
        cost_estimate=cost(12 * 10**9, 8 * 2**20, HQ * 655360),
    )(core, src, held, inc, pack, dout, after)


def keep_kernel(core_ref, attn_ref, dout_hbm, keep_ref, dout, sem):
    mine = pl.ds(pl.multiple_of(core_ref[0] * HALF, HALF), HALF)
    load = pltpu.make_async_copy(dout_hbm.at[:, mine], dout, sem)
    load.start()
    load.wait()
    keep_ref[...] = dot(attn_ref[...], dout[...], NN).astype(BF16)


def keep_half(core, attn_t, dout):
    return pl.pallas_call(
        keep_kernel,
        out_shape=shape((HQ * HD, HALF)),
        in_specs=[SMEM, VMEM, ANY],
        out_specs=VMEM,
        scratch_shapes=[pltpu.VMEM((TOK, HALF), BF16), pltpu.SemaphoreType.DMA],
        compiler_params=params(12),
        name="keep_half",
        cost_estimate=cost(2 * TOK * HALF * HQ * HD, 8 * 2**20),
    )(core, attn_t, dout)


PAIR = 2


def backward_kernel(
    rows_hbm, pack_ref, dt_hbm, attn_hbm, stat_ref, _, dq_out, kv_ref, token,
    rows, dt, attn_ref, key_t, weight_t, score_t, acc, dq, dq_sems, load_sems,
):
    token[...] = jnp.zeros(token.shape, F32)
    rows_load = pltpu.make_async_copy(rows_hbm, rows, load_sems.at[0])
    rows_load.start()
    head_loads = []
    for h in range(HQ):
        here = pl.ds(h * HD, HD)
        head_loads.append(
            [
                pltpu.make_async_copy(dt_hbm.at[here, :], dt.at[here, :], load_sems.at[2 * h + 1]),
                pltpu.make_async_copy(attn_hbm.at[here, :], attn_ref.at[here, :], load_sems.at[2 * h + 2]),
            ]
        )
        for load in head_loads[h]:
            load.start()
    start = pack_ref[...]
    rows_load.wait()
    key_t[...] = transposed(rows[:, KEY])
    stores = []
    for first in range(0, HQ, PAIR):
        heads = range(first, first + PAIR)
        for head in heads:
            for load in head_loads[head]:
                load.wait()
        steps = [(head, tile) for head in heads for tile in range(TILES)]

        def products(step):
            head, tile = step
            width = (tile + 1) * TILE
            span = slice(tile * TILE, width)
            here = slice(head * HD, (head + 1) * HD)
            return dot(rows[:width, KEY], rows[span, here], NT), dot(rows[:width, VALUE], dt[here, span], NN)

        ahead = products(steps[0])
        for n, (head, tile) in enumerate(steps):
            scores, dprob = ahead
            if n + 1 < len(steps):
                ahead = products(steps[n + 1])
            here = slice(head * HD, (head + 1) * HD)
            width = (tile + 1) * TILE
            span = slice(tile * TILE, width)
            at = (head - first) * TOK
            spot = slice(at + tile * TILE, at + width)
            delta = jnp.sum(
                dt[here, span].astype(F32) * attn_ref[here, span].astype(F32), axis=0, keepdims=True
            )
            mask = keep_mask(tile, start)
            prob = jnp.exp2(jnp.where(mask, scores * EXP2_SCALE - stat_ref[head : head + 1, span], -jnp.inf))
            weight_t[:width, spot] = prob.astype(BF16)
            dscore = (prob * (dprob - delta)).astype(BF16)
            score_t[:width, spot] = dscore
            dq_t = dot(key_t[:, :width], dscore, NN) * SCALE
            dq[head, span, :] = dq_t.T.astype(BF16)
            if tile == TILES - 1:
                store = pltpu.make_async_copy(dq.at[head], dq_out.at[:, pl.ds(head * HD, HD)], dq_sems.at[head])
                store.start()
                stores.append(store)
        for tile in range(TILES):
            span = slice(tile * TILE, (tile + 1) * TILE)
            dk = jnp.zeros((TILE, HD), F32) if first == 0 else acc[span, :HD]
            dv = jnp.zeros((TILE, HD), F32) if first == 0 else acc[span, HD:]
            for head in range(first, first + PAIR):
                here = slice(head * HD, (head + 1) * HD)
                at = (head - first) * TOK
                spot = slice(at + tile * TILE, at + TOK)
                dk = dk + dot(score_t[span, spot], rows[tile * TILE :, here], NN)
                dv = dv + dot(weight_t[span, spot], dt[here, tile * TILE :], NT)
            if first + PAIR == HQ:
                kv_ref[span, :HD] = (dk * SCALE).astype(BF16)
                kv_ref[span, HD:] = dv.astype(BF16)
            else:
                acc[span, :HD] = dk
                acc[span, HD:] = dv
    for store in stores:
        store.wait()


def backward(rows, pack, d_attn_t, attn_t, stats, after):
    return pl.pallas_call(
        backward_kernel,
        out_shape=[shape((TOK, HQ * HD)), shape((TOK, 2 * HD)), TOKEN],
        in_specs=[ANY, VMEM, ANY, ANY, VMEM, ANY],
        out_specs=[ANY, VMEM, VMEM],
        scratch_shapes=[
            pltpu.VMEM((TOK, WIDTH), BF16),
            pltpu.VMEM((HQ * HD, TOK), BF16),
            pltpu.VMEM((HQ * HD, TOK), BF16),
            pltpu.VMEM((HD, TOK), BF16),
            pltpu.VMEM((TOK, PAIR * TOK), BF16),
            pltpu.VMEM((TOK, PAIR * TOK), BF16),
            pltpu.VMEM((TOK, 2 * HD), F32),
            pltpu.VMEM((HQ, TOK, HD), BF16),
            pltpu.SemaphoreType.DMA((HQ,)),
            pltpu.SemaphoreType.DMA((2 * HQ + 1,)),
        ],
        compiler_params=params(LARGE),
        name="backward",
        cost_estimate=cost(30 * 10**9, 8 * 2**20, HQ * 655360),
    )(rows, pack, d_attn_t, attn_t, stats, after)


def add_pair_kernel(x_ref, keep_ref, got_ref, *outs):
    *outs, token = outs
    token[...] = jnp.zeros(token.shape, F32)
    x = x_ref[0]
    for k, out in enumerate(outs):
        shard = lax.rem(x + k, N_FSDP)
        out[...] = (keep_ref[shard].astype(F32) + got_ref[shard].astype(F32)).astype(out.dtype)


def add_pair(x, keep, got):
    rows = keep.shape[0] // N_FSDP
    dims = (rows, HALF)
    return pl.pallas_call(
        add_pair_kernel,
        out_shape=[shape(dims, F32)] + [shape(dims)] * 3 + [TOKEN],
        in_specs=[SMEM, VMEM, VMEM],
        out_specs=[VMEM] * 5,
        compiler_params=params(4),
        name="add_pair",
        cost_estimate=cost(4 * rows * HALF, 10 * rows * HALF * 2),
    )(x, keep.reshape(N_FSDP, *dims), got.reshape(N_FSDP, *dims))


def sum4(parts):
    total = parts[0].astype(F32)
    for part in parts[1:]:
        total = total + part.astype(F32)
    return total


def split_z_kernel(z_ref, _, *refs):
    parts, outs, total = refs[:4], refs[4:8], refs[8]
    total[...] = sum4([r[...] for r in parts])
    size = SHARD // 4
    z = z_ref[0]
    for k, out in enumerate(outs):
        at = pl.multiple_of(lax.rem(z + k, 4) * size, size)
        out[...] = total[pl.ds(at, size), :].astype(out.dtype)


def split_z(z, after, parts):
    dims = (SHARD // 4, HALF)
    return pl.pallas_call(
        split_z_kernel,
        out_shape=[shape(dims, F32)] + [shape(dims)] * 3,
        in_specs=[SMEM, ANY] + [VMEM] * 4,
        out_specs=[VMEM] * 4,
        scratch_shapes=[pltpu.VMEM((SHARD, HALF), F32)],
        compiler_params=params(4),
        name="split_z",
        cost_estimate=cost(4 * SHARD * HALF, 10 * SHARD * HALF),
    )(z, after, *parts)


def sum4_kernel(factor, *refs):
    refs[4][...] = (sum4([r[...] for r in refs[:4]]) * factor).astype(BF16)


def sum_four(parts, factor=1.0):
    return pl.pallas_call(
        functools.partial(sum4_kernel, factor),
        out_shape=shape(parts[0].shape),
        in_specs=[VMEM] * 4,
        out_specs=VMEM,
        compiler_params=params(8),
        name="sum_four",
        cost_estimate=cost(4 * parts[0].size, 10 * parts[0].size),
    )(*parts)


def join_z_kernel(z_ref, *refs):
    parts, out = refs[:4], refs[4]
    size = SHARD // 4
    for k, ref in enumerate(parts):
        at = pl.multiple_of(lax.rem(z_ref[0] - k + 4, 4) * size, size)
        out[pl.ds(at, size), :] = ref[...]


def join_z(z, parts):
    return pl.pallas_call(
        join_z_kernel,
        out_shape=shape((SHARD, HALF)),
        in_specs=[SMEM] + [VMEM] * 4,
        out_specs=VMEM,
        compiler_params=params(4),
        name="join_z",
        cost_estimate=cost(0, 4 * SHARD * HALF),
    )(z, *parts)


def lay_out_kernel(core_ref, own, got, out):
    for part, side in ((own, core_ref[0]), (got, 1 - core_ref[0])):
        columns = pl.ds(pl.multiple_of(side * HALF, HALF), HALF)
        out[:, columns] = part[...].astype(F32)


def lay_out(core, own, got):
    return pl.pallas_call(
        lay_out_kernel,
        out_shape=shape((SHARD, D), F32),
        in_specs=[SMEM, VMEM, VMEM],
        out_specs=VMEM,
        compiler_params=params(4),
        name="lay_out",
        cost_estimate=cost(SHARD * D, 6 * SHARD * D),
    )(core, own, got)


def dp_shift(dy, dz, dc):
    pairs = []
    for i in range(32):
        y, z, c = i // 8, (i // 2) % 4, i % 2
        pairs.append((i, ((y + dy) % 4) * 8 + ((z + dz) % 4) * 2 + (c + dc) % 2))
    return pairs


def x_shift(k):
    return [(i, (i + k) % N_FSDP) for i in range(N_FSDP)]


def per_device(stash, stash_place, pack_start, d_out, out_weight):
    group = lax.axis_index("dp")
    x = lax.axis_index("fsdp")
    core = lax.rem(group, 2)
    z = lax.rem(group // 2, 4)
    held = stash.reshape(NB, BLK, WIDTH)
    peers = jnp.arange(NB, dtype=jnp.int32)
    holder = stash_place // NB
    slot = stash_place % NB
    chosen = jnp.sum(jnp.where((holder == group) & (peers[:, None] != group), slot, 0), axis=1)
    mine = lax.dynamic_index_in_dim(stash_place, group, 0, keepdims=False)
    source = jnp.where(mine // NB == group, mine % NB, NB + mine // NB)
    x1, z1, core1 = x.reshape(1), z.reshape(1), core.reshape(1)

    incoming = lax.all_to_all(held[chosen], "dp", split_axis=0, concat_axis=0, tiled=True)
    swap = dp_shift(0, 0, 1)
    half = lax.dynamic_slice_in_dim(out_weight, core * HALF, HALF, 1)
    weight_mine = [lax.ppermute(half, "fsdp", x_shift(k)) for k in (1, 2, 3)]
    weight_other = [lax.ppermute(part, "dp", swap) for part in weight_mine]
    d_attn_t = d_attn_transposed(jnp.stack([x, core]), out_weight, weight_mine, weight_other, d_out)

    pack = pack_start.reshape(1, TOK)
    rows, attn_t, stats, send = forward(core1, source, held, incoming, pack, d_out, d_attn_t)
    keep = keep_half(core1, attn_t, d_out)
    *parts, x_token = add_pair(x1, keep, lax.ppermute(send, "dp", swap))
    by_x = [parts[0]] + [lax.ppermute(parts[k], "fsdp", x_shift(k)) for k in (1, 2, 3)]
    grad_query, grad_keyval, token = backward(rows, pack, d_attn_t, attn_t, stats, x_token)
    by_z = split_z(z1, token, by_x)
    by_z = [by_z[0]] + [lax.ppermute(by_z[k], "dp", dp_shift(0, k, 0)) for k in (1, 2, 3)]
    z_sum = sum_four(by_z)
    by_y = [z_sum] + [lax.ppermute(z_sum, "dp", dp_shift(k, 0, 0)) for k in (1, 2, 3)]
    factor = (TOK * lax.axis_size("dp") * lax.axis_size("fsdp")) ** (-0.5)
    total = sum_four(by_y, factor)
    own = join_z(z1, [total] + [lax.ppermute(total, "dp", dp_shift(0, k, 0)) for k in (1, 2, 3)])
    grad_weight = lay_out(core1, own, lax.ppermute(own, "dp", swap))
    return (grad_query, grad_keyval, grad_weight)


def solution(mesh):
    in_specs = (
        P("dp", "fsdp", None, None, None),
        P(),
        P(("dp", "fsdp")),
        P(("dp", "fsdp"), None),
        P("fsdp", None),
    )
    out_specs = (P(("dp", "fsdp"), None), P(("dp", "fsdp"), None), P("fsdp", None))
    return jax.shard_map(
        per_device, mesh=mesh, in_specs=in_specs, out_specs=out_specs, check_vma=False
    )
```

```python
import functools

import jax
import jax.numpy as jnp
from jax import lax
from jax.experimental import pallas as pl
from jax.experimental.pallas import tpu as pltpu
from jax.sharding import PartitionSpec as P

HQ = 6
HD = 128
TILE = 256
TOK = 1024
TILES = TOK // TILE
D = 1536
HALF = D // 2
NB = 32
BLK = 32
WIDTH = 1024
N_FSDP = 4
SHARD = HQ * HD // N_FSDP
SCALE = HD ** (-0.5)
EXP2_SCALE = SCALE * 1.4426950408889634
KEY = slice(HQ * HD, (HQ + 1) * HD)
VALUE = slice((HQ + 1) * HD, (HQ + 2) * HD)
NT = (((1,), (1,)), ((), ()))
NN = (((1,), (0,)), ((), ()))
ANY = pl.BlockSpec(memory_space=pl.ANY)
SMEM = pl.BlockSpec(memory_space=pltpu.SMEM)
VMEM = pl.BlockSpec(memory_space=pltpu.VMEM)
HBM = pl.BlockSpec(memory_space=pltpu.HBM)


def params(mib):
    return pltpu.CompilerParams(vmem_limit_bytes=mib * 2**20)


BF16 = jnp.bfloat16
LARGE = 56
F32 = jnp.float32


def dot(a, b, dims):
    return lax.dot_general(a, b, dims, preferred_element_type=F32)


def shape(dims, dtype=BF16):
    return jax.ShapeDtypeStruct(dims, dtype)


TOKEN = shape((8, 128), F32)


def cost(flops, size, exps=0):
    return pl.CostEstimate(flops=int(flops), bytes_accessed=int(size), transcendentals=int(exps))


def d_attn_kernel(pos_ref, *refs):
    own, mine, others, dout, out_ref, weight, sems = (
        refs[0], refs[1:4], refs[4:7], *refs[7:]
    )
    x, core = pos_ref[0], pos_ref[1]

    def shard_rows(k):
        return pl.ds(pl.multiple_of(lax.rem(x - k + N_FSDP, N_FSDP) * SHARD, SHARD), SHARD)

    loads = [pltpu.make_async_copy(own, weight.at[shard_rows(0), :], sems.at[0])]
    for k in range(1, N_FSDP):
        for i, (part, side) in enumerate(((mine[k - 1], core), (others[k - 1], 1 - core))):
            columns = pl.ds(pl.multiple_of(side * HALF, HALF), HALF)
            loads.append(pltpu.make_async_copy(part, weight.at[shard_rows(k), columns], sems.at[2 * k - 1 + i]))
    for load in loads:
        load.start()
    for load in loads:
        load.wait()
    out_ref[...] = dot(weight[...], dout[...], NT).astype(BF16)


def d_attn_transposed(pos, own, mine, others, dout):
    return pl.pallas_call(
        d_attn_kernel,
        out_shape=shape((HQ * HD, TOK)),
        in_specs=[SMEM] + [ANY] * 7 + [VMEM],
        out_specs=VMEM,
        scratch_shapes=[pltpu.VMEM((HQ * HD, D), BF16), pltpu.SemaphoreType.DMA((7,))],
        compiler_params=params(10),
        name="d_attn",
        cost_estimate=cost(2 * TOK * D * HQ * HD, 8 * 2**20),
    )(pos, own, *mine, *others, dout)


TRIO = 3


def keep_mask(tile, start):
    width = (tile + 1) * TILE
    key = lax.broadcasted_iota(jnp.int32, (width, TILE), 0)
    query = tile * TILE + lax.broadcasted_iota(jnp.int32, (width, TILE), 1)
    return (key >= start[:, tile * TILE : width]) & (key <= query)


def transposed(x):
    return x.astype(F32).T.astype(BF16)


def gather_rows(src_ref, held_ref, inc_ref, rows, sems):
    def copy(ref, b, source):
        return pltpu.make_async_copy(ref.at[source], rows.at[pl.ds(b * BLK, BLK), :], sems.at[b])

    for b in range(NB):
        source = src_ref[b]

        @pl.when(source < NB)
        def _(b=b, source=source):
            copy(held_ref, b, source).start()

        @pl.when(source >= NB)
        def _(b=b, source=source):
            copy(inc_ref, b, source - NB).start()

    def wait_rows(tile):
        per_tile = TILE // BLK
        for b in range(tile * per_tile, (tile + 1) * per_tile):
            copy(held_ref, b, 0).wait()

    return wait_rows


def forward_kernel(
    core_ref, src_ref, held_ref, inc_ref, pack_ref, dout_hbm, _,
    rows_out, attn_out, stat_ref, send_out,
    rows, attn_ref, send_ref, dout, value_t, sems, side_sems, attn_sems,
):
    wait_rows = gather_rows(src_ref, held_ref, inc_ref, rows, sems)
    other = pl.ds(pl.multiple_of((1 - core_ref[0]) * HALF, HALF), HALF)
    dout_copy = pltpu.make_async_copy(dout_hbm.at[:, other], dout, side_sems.at[0])
    dout_copy.start()
    rows_copy = pltpu.make_async_copy(rows, rows_out, side_sems.at[1])
    send_copy = pltpu.make_async_copy(send_ref, send_out, side_sems.at[2])
    attn_copies = [
        pltpu.make_async_copy(
            attn_ref.at[pl.ds(h * HD, HD), :], attn_out.at[pl.ds(h * HD, HD), :], attn_sems.at[h]
        )
        for h in range(HQ)
    ]
    start = pack_ref[...]
    for tile in range(TILES):
        width = (tile + 1) * TILE
        span = slice(tile * TILE, width)
        wait_rows(tile)
        if tile == TILES - 1:
            rows_copy.start()
        value_t[:, span] = transposed(rows[span, VALUE])
        masks = jnp.concatenate([keep_mask(tile, start)] * TRIO, axis=1)

        def raw_scores(first, width=width, span=span):
            query = jnp.concatenate(
                [rows[span, h * HD : (h + 1) * HD] for h in range(first, first + TRIO)], axis=0
            )
            return dot(rows[:width, KEY], query, NT)

        ahead = raw_scores(0)
        for first in range(0, HQ, TRIO):
            scores = ahead
            if first + TRIO < HQ:
                ahead = raw_scores(first + TRIO)
            scores = jnp.where(masks, scores, -jnp.inf)
            top = jnp.max(scores, axis=0, keepdims=True)
            expo = jnp.exp2((scores - top) * EXP2_SCALE)
            total = jnp.sum(expo, axis=0, keepdims=True)
            attn = (dot(value_t[:, :width], expo.astype(BF16), NN) * (1.0 / total)).astype(BF16)
            stat = top * EXP2_SCALE + jnp.log2(total)
            for k in range(TRIO):
                part = slice(k * TILE, (k + 1) * TILE)
                attn_ref[(first + k) * HD : (first + k + 1) * HD, span] = attn[:, part]
                stat_ref[first + k : first + k + 1, span] = stat[:, part]
    for copy in attn_copies:
        copy.start()
    dout_copy.wait()
    send_ref[...] = dot(attn_ref[...], dout[...], NN).astype(BF16)
    send_copy.start()
    for copy in (rows_copy, *attn_copies, send_copy):
        copy.wait()


def forward(core, src, held, inc, pack, dout, after):
    n = HQ * HD
    return pl.pallas_call(
        forward_kernel,
        out_shape=[
            shape((TOK, WIDTH)), shape((n, TOK)), shape((8, TOK), F32), shape((n, HALF))
        ],
        in_specs=[SMEM, SMEM, ANY, ANY, VMEM, ANY, ANY],
        out_specs=[ANY, ANY, VMEM, ANY],
        scratch_shapes=[
            pltpu.VMEM((TOK, WIDTH), BF16),
            pltpu.VMEM((n, TOK), BF16),
            pltpu.VMEM((n, HALF), BF16),
            pltpu.VMEM((TOK, HALF), BF16),
            pltpu.VMEM((HD, TOK), BF16),
            pltpu.SemaphoreType.DMA((NB,)),
            pltpu.SemaphoreType.DMA((3,)),
            pltpu.SemaphoreType.DMA((HQ,)),
        ],
        compiler_params=params(LARGE),
        name="forward",
        cost_estimate=cost(12 * 10**9, 8 * 2**20, HQ * 655360),
    )(core, src, held, inc, pack, dout, after)


def keep_kernel(core_ref, attn_ref, dout_hbm, keep_ref, dout, sem):
    mine = pl.ds(pl.multiple_of(core_ref[0] * HALF, HALF), HALF)
    load = pltpu.make_async_copy(dout_hbm.at[:, mine], dout, sem)
    load.start()
    load.wait()
    keep_ref[...] = dot(attn_ref[...], dout[...], NN).astype(BF16)


def keep_half(core, attn_t, dout):
    return pl.pallas_call(
        keep_kernel,
        out_shape=shape((HQ * HD, HALF)),
        in_specs=[SMEM, VMEM, ANY],
        out_specs=VMEM,
        scratch_shapes=[pltpu.VMEM((TOK, HALF), BF16), pltpu.SemaphoreType.DMA],
        compiler_params=params(12),
        name="keep_half",
        cost_estimate=cost(2 * TOK * HALF * HQ * HD, 8 * 2**20),
    )(core, attn_t, dout)


PAIR = 2


def backward_kernel(
    rows, pack_ref, dt, attn_ref, stat_ref, _, dq_out, kv_ref, token,
    key_t, weight_t, score_t, acc, dq, dq_sems,
):
    token[...] = jnp.zeros(token.shape, F32)
    start = pack_ref[...]
    key_t[...] = transposed(rows[:, KEY])
    stores = []
    for first in range(0, HQ, PAIR):
        heads = range(first, first + PAIR)
        steps = [(head, tile) for head in heads for tile in range(TILES)]

        def products(step):
            head, tile = step
            width = (tile + 1) * TILE
            span = slice(tile * TILE, width)
            here = slice(head * HD, (head + 1) * HD)
            return dot(rows[:width, KEY], rows[span, here], NT), dot(rows[:width, VALUE], dt[here, span], NN)

        ahead = products(steps[0])
        for n, (head, tile) in enumerate(steps):
            scores, dprob = ahead
            if n + 1 < len(steps):
                ahead = products(steps[n + 1])
            here = slice(head * HD, (head + 1) * HD)
            width = (tile + 1) * TILE
            span = slice(tile * TILE, width)
            at = (head - first) * TOK
            spot = slice(at + tile * TILE, at + width)
            delta = jnp.sum(
                dt[here, span].astype(F32) * attn_ref[here, span].astype(F32), axis=0, keepdims=True
            )
            mask = keep_mask(tile, start)
            prob = jnp.exp2(jnp.where(mask, scores * EXP2_SCALE - stat_ref[head : head + 1, span], -jnp.inf))
            weight_t[:width, spot] = prob.astype(BF16)
            dscore = (prob * (dprob - delta)).astype(BF16)
            score_t[:width, spot] = dscore
            dq_t = dot(key_t[:, :width], dscore, NN) * SCALE
            dq[head, span, :] = dq_t.T.astype(BF16)
            if tile == TILES - 1:
                store = pltpu.make_async_copy(dq.at[head], dq_out.at[:, pl.ds(head * HD, HD)], dq_sems.at[head])
                store.start()
                stores.append(store)
        for tile in range(TILES):
            span = slice(tile * TILE, (tile + 1) * TILE)
            dk = jnp.zeros((TILE, HD), F32) if first == 0 else acc[span, :HD]
            dv = jnp.zeros((TILE, HD), F32) if first == 0 else acc[span, HD:]
            for head in range(first, first + PAIR):
                here = slice(head * HD, (head + 1) * HD)
                at = (head - first) * TOK
                spot = slice(at + tile * TILE, at + TOK)
                dk = dk + dot(score_t[span, spot], rows[tile * TILE :, here], NN)
                dv = dv + dot(weight_t[span, spot], dt[here, tile * TILE :], NT)
            if first + PAIR == HQ:
                kv_ref[span, :HD] = (dk * SCALE).astype(BF16)
                kv_ref[span, HD:] = dv.astype(BF16)
            else:
                acc[span, :HD] = dk
                acc[span, HD:] = dv
    for store in stores:
        store.wait()


def backward(rows, pack, d_attn_t, attn_t, stats, after):
    return pl.pallas_call(
        backward_kernel,
        out_shape=[shape((TOK, HQ * HD)), shape((TOK, 2 * HD)), TOKEN],
        in_specs=[VMEM] * 5 + [ANY],
        out_specs=[ANY, VMEM, VMEM],
        scratch_shapes=[
            pltpu.VMEM((HD, TOK), BF16),
            pltpu.VMEM((TOK, PAIR * TOK), BF16),
            pltpu.VMEM((TOK, PAIR * TOK), BF16),
            pltpu.VMEM((TOK, 2 * HD), F32),
            pltpu.VMEM((HQ, TOK, HD), BF16),
            pltpu.SemaphoreType.DMA((HQ,)),
        ],
        compiler_params=params(24),
        name="backward",
        cost_estimate=cost(30 * 10**9, 8 * 2**20, HQ * 655360),
    )(rows, pack, d_attn_t, attn_t, stats, after)


def add_pair_kernel(x_ref, keep_ref, got_hbm, *outs):
    *outs, token, got_ref, sems = outs
    loads = [pltpu.make_async_copy(got_hbm.at[k], got_ref.at[k], sems.at[k]) for k in range(N_FSDP)]
    for load in loads:
        load.start()
    for load in loads:
        load.wait()
    token[...] = jnp.zeros(token.shape, F32)
    x = x_ref[0]
    for k, out in enumerate(outs):
        shard = lax.rem(x + k, N_FSDP)
        out[...] = (keep_ref[shard].astype(F32) + got_ref[shard].astype(F32)).astype(out.dtype)


def add_pair(x, keep, got):
    rows = keep.shape[0] // N_FSDP
    dims = (rows, HALF)
    return pl.pallas_call(
        add_pair_kernel,
        out_shape=[shape(dims, F32)] + [shape(dims)] * 3 + [TOKEN],
        in_specs=[SMEM, VMEM, ANY],
        out_specs=[VMEM] * 5,
        scratch_shapes=[pltpu.VMEM((N_FSDP, *dims), BF16), pltpu.SemaphoreType.DMA((N_FSDP,))],
        compiler_params=params(4),
        name="add_pair",
        cost_estimate=cost(4 * rows * HALF, 10 * rows * HALF * 2),
    )(x, keep.reshape(N_FSDP, *dims), got.reshape(N_FSDP, *dims))


def sum4(parts):
    total = parts[0].astype(F32)
    for part in parts[1:]:
        total = total + part.astype(F32)
    return total


def split_z_kernel(z_ref, _, *refs):
    parts, outs, total = refs[:4], refs[4:8], refs[8]
    total[...] = sum4([r[...] for r in parts])
    size = SHARD // 4
    z = z_ref[0]
    for k, out in enumerate(outs):
        at = pl.multiple_of(lax.rem(z + k, 4) * size, size)
        out[...] = total[pl.ds(at, size), :].astype(out.dtype)


def split_z(z, after, parts):
    dims = (SHARD // 4, HALF)
    return pl.pallas_call(
        split_z_kernel,
        out_shape=[shape(dims, F32)] + [shape(dims)] * 3,
        in_specs=[SMEM, ANY] + [VMEM] * 4,
        out_specs=[VMEM] * 4,
        scratch_shapes=[pltpu.VMEM((SHARD, HALF), F32)],
        compiler_params=params(4),
        name="split_z",
        cost_estimate=cost(4 * SHARD * HALF, 10 * SHARD * HALF),
    )(z, after, *parts)


def sum4_kernel(factor, *refs):
    refs[4][...] = (sum4([r[...] for r in refs[:4]]) * factor).astype(BF16)


def sum_four(parts, factor=1.0):
    return pl.pallas_call(
        functools.partial(sum4_kernel, factor),
        out_shape=shape(parts[0].shape),
        in_specs=[VMEM] * 4,
        out_specs=VMEM,
        compiler_params=params(8),
        name="sum_four",
        cost_estimate=cost(4 * parts[0].size, 10 * parts[0].size),
    )(*parts)


def join_z_kernel(z_ref, *refs):
    parts, out = refs[:4], refs[4]
    size = SHARD // 4
    for k, ref in enumerate(parts):
        at = pl.multiple_of(lax.rem(z_ref[0] - k + 4, 4) * size, size)
        out[pl.ds(at, size), :] = ref[...]


def join_z(z, parts):
    return pl.pallas_call(
        join_z_kernel,
        out_shape=shape((SHARD, HALF)),
        in_specs=[SMEM] + [VMEM] * 4,
        out_specs=VMEM,
        compiler_params=params(4),
        name="join_z",
        cost_estimate=cost(0, 4 * SHARD * HALF),
    )(z, *parts)


def lay_out_kernel(core_ref, own, got, out):
    for part, side in ((own, core_ref[0]), (got, 1 - core_ref[0])):
        columns = pl.ds(pl.multiple_of(side * HALF, HALF), HALF)
        out[:, columns] = part[...].astype(F32)


def lay_out(core, own, got):
    return pl.pallas_call(
        lay_out_kernel,
        out_shape=shape((SHARD, D), F32),
        in_specs=[SMEM, VMEM, VMEM],
        out_specs=VMEM,
        compiler_params=params(4),
        name="lay_out",
        cost_estimate=cost(SHARD * D, 6 * SHARD * D),
    )(core, own, got)


def dp_shift(dy, dz, dc):
    pairs = []
    for i in range(32):
        y, z, c = i // 8, (i // 2) % 4, i % 2
        pairs.append((i, ((y + dy) % 4) * 8 + ((z + dz) % 4) * 2 + (c + dc) % 2))
    return pairs


def x_shift(k):
    return [(i, (i + k) % N_FSDP) for i in range(N_FSDP)]


def per_device(stash, stash_place, pack_start, d_out, out_weight):
    group = lax.axis_index("dp")
    x = lax.axis_index("fsdp")
    core = lax.rem(group, 2)
    z = lax.rem(group // 2, 4)
    held = stash.reshape(NB, BLK, WIDTH)
    peers = jnp.arange(NB, dtype=jnp.int32)
    holder = stash_place // NB
    slot = stash_place % NB
    chosen = jnp.sum(jnp.where((holder == group) & (peers[:, None] != group), slot, 0), axis=1)
    mine = lax.dynamic_index_in_dim(stash_place, group, 0, keepdims=False)
    source = jnp.where(mine // NB == group, mine % NB, NB + mine // NB)
    x1, z1, core1 = x.reshape(1), z.reshape(1), core.reshape(1)

    incoming = lax.all_to_all(held[chosen], "dp", split_axis=0, concat_axis=0, tiled=True)
    swap = dp_shift(0, 0, 1)
    half = lax.dynamic_slice_in_dim(out_weight, core * HALF, HALF, 1)
    weight_mine = [lax.ppermute(half, "fsdp", x_shift(k)) for k in (1, 2, 3)]
    weight_other = [lax.ppermute(part, "dp", swap) for part in weight_mine]
    d_attn_t = d_attn_transposed(jnp.stack([x, core]), out_weight, weight_mine, weight_other, d_out)

    pack = pack_start.reshape(1, TOK)
    rows, attn_t, stats, send = forward(core1, source, held, incoming, pack, d_out, d_attn_t)
    keep = keep_half(core1, attn_t, d_out)
    *parts, x_token = add_pair(x1, keep, lax.ppermute(send, "dp", swap))
    by_x = [parts[0]] + [lax.ppermute(parts[k], "fsdp", x_shift(k)) for k in (2, 1, 3)]
    grad_query, grad_keyval, token = backward(rows, pack, d_attn_t, attn_t, stats, x_token)
    by_z = split_z(z1, token, by_x)
    by_z = [by_z[0]] + [lax.ppermute(by_z[k], "dp", dp_shift(0, k, 0)) for k in (2, 1, 3)]
    z_sum = sum_four(by_z)
    by_y = [z_sum] + [lax.ppermute(z_sum, "dp", dp_shift(k, 0, 0)) for k in (1, 3, 2)]
    factor = (TOK * lax.axis_size("dp") * lax.axis_size("fsdp")) ** (-0.5)
    total = sum_four(by_y, factor)
    by_z = {k: lax.ppermute(total, "dp", dp_shift(0, k, 0)) for k in (1, 3, 2)}
    own = join_z(z1, [total] + [by_z[k] for k in (1, 2, 3)])
    grad_weight = lay_out(core1, own, lax.ppermute(own, "dp", swap))
    return (grad_query, grad_keyval, grad_weight)


def solution(mesh):
    in_specs = (
        P("dp", "fsdp", None, None, None),
        P(),
        P(("dp", "fsdp")),
        P(("dp", "fsdp"), None),
        P("fsdp", None),
    )
    out_specs = (P(("dp", "fsdp"), None), P(("dp", "fsdp"), None), P("fsdp", None))
    return jax.shard_map(
        per_device, mesh=mesh, in_specs=in_specs, out_specs=out_specs, check_vma=False
    )
```

```python
import functools

import jax
import jax.numpy as jnp
from jax import lax
from jax.experimental import pallas as pl
from jax.experimental.pallas import tpu as pltpu
from jax.sharding import PartitionSpec as P

HQ = 6
HD = 128
TILE = 256
TOK = 1024
TILES = TOK // TILE
D = 1536
HALF = D // 2
NB = 32
BLK = 32
WIDTH = 1024
N_FSDP = 4
SHARD = HQ * HD // N_FSDP
SCALE = HD ** (-0.5)
EXP2_SCALE = SCALE * 1.4426950408889634
KEY = slice(HQ * HD, (HQ + 1) * HD)
VALUE = slice((HQ + 1) * HD, (HQ + 2) * HD)
NT = (((1,), (1,)), ((), ()))
NN = (((1,), (0,)), ((), ()))
ANY = pl.BlockSpec(memory_space=pl.ANY)
SMEM = pl.BlockSpec(memory_space=pltpu.SMEM)
VMEM = pl.BlockSpec(memory_space=pltpu.VMEM)
HBM = pl.BlockSpec(memory_space=pltpu.HBM)


def params(mib):
    return pltpu.CompilerParams(vmem_limit_bytes=mib * 2**20)


BF16 = jnp.bfloat16
LARGE = 56
F32 = jnp.float32


def dot(a, b, dims):
    return lax.dot_general(a, b, dims, preferred_element_type=F32)


def shape(dims, dtype=BF16):
    return jax.ShapeDtypeStruct(dims, dtype)


TOKEN = shape((8, 128), F32)


def cost(flops, size, exps=0):
    return pl.CostEstimate(flops=int(flops), bytes_accessed=int(size), transcendentals=int(exps))


def d_attn_kernel(x_ref, core_ref, *refs):
    own, mine, others, dout, out_ref, weight, sems = (
        refs[0], refs[1:4], refs[4:7], *refs[7:]
    )
    x, core = x_ref[0], core_ref[0]

    def shard_rows(k):
        return pl.ds(pl.multiple_of(lax.rem(x - k + N_FSDP, N_FSDP) * SHARD, SHARD), SHARD)

    loads = [pltpu.make_async_copy(own, weight.at[shard_rows(0), :], sems.at[0])]
    for k in range(1, N_FSDP):
        for i, (part, side) in enumerate(((mine[k - 1], core), (others[k - 1], 1 - core))):
            columns = pl.ds(pl.multiple_of(side * HALF, HALF), HALF)
            loads.append(pltpu.make_async_copy(part, weight.at[shard_rows(k), columns], sems.at[2 * k - 1 + i]))
    for load in loads:
        load.start()
    for load in loads:
        load.wait()
    out_ref[...] = dot(weight[...], dout[...], NT).astype(BF16)


def d_attn_transposed(x, core, own, mine, others, dout):
    return pl.pallas_call(
        d_attn_kernel,
        out_shape=shape((HQ * HD, TOK)),
        in_specs=[SMEM, SMEM] + [ANY] * 7 + [VMEM],
        out_specs=VMEM,
        scratch_shapes=[pltpu.VMEM((HQ * HD, D), BF16), pltpu.SemaphoreType.DMA((7,))],
        compiler_params=params(10),
        name="d_attn",
        cost_estimate=cost(2 * TOK * D * HQ * HD, 8 * 2**20),
    )(x, core, own, *mine, *others, dout)


TRIO = 3


def keep_mask(tile, start):
    width = (tile + 1) * TILE
    key = lax.broadcasted_iota(jnp.int32, (width, TILE), 0)
    query = tile * TILE + lax.broadcasted_iota(jnp.int32, (width, TILE), 1)
    return (key >= start[:, tile * TILE : width]) & (key <= query)


def transposed(x):
    return x.astype(F32).T.astype(BF16)


def gather_rows(group, place_ref, held_ref, inc_ref, rows, sems):
    def copy(ref, b, source):
        return pltpu.make_async_copy(ref.at[source], rows.at[pl.ds(b * BLK, BLK), :], sems.at[b])

    for b in range(NB):
        place = place_ref[group, b]
        holder = lax.shift_right_logical(place, 5)
        slot = place - holder * NB

        @pl.when(holder == group)
        def _(b=b, slot=slot):
            copy(held_ref, b, slot).start()

        @pl.when(holder != group)
        def _(b=b, holder=holder):
            copy(inc_ref, b, holder).start()

    def wait_rows(tile):
        per_tile = TILE // BLK
        for b in range(tile * per_tile, (tile + 1) * per_tile):
            copy(held_ref, b, 0).wait()

    return wait_rows


def forward_kernel(
    group_ref, place_ref, held_ref, inc_ref, pack_ref, dout_hbm, _,
    rows_out, attn_out, stat_ref, send_out,
    rows, attn_ref, send_ref, dout, value_t, sems, side_sems, attn_sems,
):
    group = group_ref[0]
    wait_rows = gather_rows(group, place_ref, held_ref, inc_ref, rows, sems)
    other = pl.ds(pl.multiple_of((1 - lax.rem(group, 2)) * HALF, HALF), HALF)
    dout_copy = pltpu.make_async_copy(dout_hbm.at[:, other], dout, side_sems.at[0])
    dout_copy.start()
    rows_copy = pltpu.make_async_copy(rows, rows_out, side_sems.at[1])
    send_copies = [
        pltpu.make_async_copy(
            send_ref.at[pl.ds(half * (HQ * HD // 2), HQ * HD // 2), :],
            send_out.at[pl.ds(half * (HQ * HD // 2), HQ * HD // 2), :],
            side_sems.at[2 + half],
        )
        for half in range(2)
    ]
    attn_copies = [
        pltpu.make_async_copy(
            attn_ref.at[pl.ds(h * HD, HD), :], attn_out.at[pl.ds(h * HD, HD), :], attn_sems.at[h]
        )
        for h in range(HQ)
    ]
    start = pack_ref[...]
    for tile in range(TILES):
        width = (tile + 1) * TILE
        span = slice(tile * TILE, width)
        wait_rows(tile)
        if tile == TILES - 1:
            rows_copy.start()
        value_t[:, span] = transposed(rows[span, VALUE])
        masks = jnp.concatenate([keep_mask(tile, start)] * TRIO, axis=1)

        def raw_scores(first, width=width, span=span):
            query = jnp.concatenate(
                [rows[span, h * HD : (h + 1) * HD] for h in range(first, first + TRIO)], axis=0
            )
            return dot(rows[:width, KEY], query, NT)

        ahead = raw_scores(0)
        for first in range(0, HQ, TRIO):
            scores = ahead
            if first + TRIO < HQ:
                ahead = raw_scores(first + TRIO)
            scores = jnp.where(masks, scores, -jnp.inf)
            top = jnp.max(scores, axis=0, keepdims=True)
            expo = jnp.exp2((scores - top) * EXP2_SCALE)
            total = jnp.sum(expo, axis=0, keepdims=True)
            attn = (dot(value_t[:, :width], expo.astype(BF16), NN) * (1.0 / total)).astype(BF16)
            stat = top * EXP2_SCALE + jnp.log2(total)
            for k in range(TRIO):
                part = slice(k * TILE, (k + 1) * TILE)
                attn_ref[(first + k) * HD : (first + k + 1) * HD, span] = attn[:, part]
                stat_ref[first + k : first + k + 1, span] = stat[:, part]
    for copy in attn_copies:
        copy.start()
    dout_copy.wait()
    for half, copy in enumerate(send_copies):
        part = slice(half * (HQ * HD // 2), (half + 1) * (HQ * HD // 2))
        send_ref[part, :] = dot(attn_ref[part, :], dout[...], NN).astype(BF16)
        copy.start()
    for copy in (rows_copy, *attn_copies, *send_copies):
        copy.wait()


def forward(group, place, held, inc, pack, dout, after):
    n = HQ * HD
    return pl.pallas_call(
        forward_kernel,
        out_shape=[
            shape((TOK, WIDTH)), shape((n, TOK)), shape((8, TOK), F32), shape((n, HALF))
        ],
        in_specs=[SMEM, SMEM, ANY, ANY, VMEM, ANY, ANY],
        out_specs=[ANY, ANY, VMEM, ANY],
        scratch_shapes=[
            pltpu.VMEM((TOK, WIDTH), BF16),
            pltpu.VMEM((n, TOK), BF16),
            pltpu.VMEM((n, HALF), BF16),
            pltpu.VMEM((TOK, HALF), BF16),
            pltpu.VMEM((HD, TOK), BF16),
            pltpu.SemaphoreType.DMA((NB,)),
            pltpu.SemaphoreType.DMA((4,)),
            pltpu.SemaphoreType.DMA((HQ,)),
        ],
        compiler_params=params(LARGE),
        name="forward",
        cost_estimate=cost(12 * 10**9, 8 * 2**20, HQ * 655360),
    )(group, place, held, inc, pack, dout, after)


def keep_kernel(core_ref, attn_ref, dout_hbm, keep_ref, dout, sem):
    mine = pl.ds(pl.multiple_of(core_ref[0] * HALF, HALF), HALF)
    load = pltpu.make_async_copy(dout_hbm.at[:, mine], dout, sem)
    load.start()
    load.wait()
    keep_ref[...] = dot(attn_ref[...], dout[...], NN).astype(BF16)


def keep_half(core, attn_t, dout):
    return pl.pallas_call(
        keep_kernel,
        out_shape=shape((HQ * HD, HALF)),
        in_specs=[SMEM, VMEM, ANY],
        out_specs=VMEM,
        scratch_shapes=[pltpu.VMEM((TOK, HALF), BF16), pltpu.SemaphoreType.DMA],
        compiler_params=params(12),
        name="keep_half",
        cost_estimate=cost(2 * TOK * HALF * HQ * HD, 8 * 2**20),
    )(core, attn_t, dout)


PAIR = 2


def backward_kernel(
    rows, pack_ref, dt, attn_ref, stat_ref, _, dq_out, kv_ref, token,
    key_t, weight_t, score_t, acc, dq, dq_sems,
):
    token[...] = jnp.zeros(token.shape, F32)
    start = pack_ref[...]
    key_t[...] = transposed(rows[:, KEY])
    stores = []
    for first in range(0, HQ, PAIR):
        heads = range(first, first + PAIR)
        steps = [(head, tile) for head in heads for tile in range(TILES)]

        def products(step):
            head, tile = step
            width = (tile + 1) * TILE
            span = slice(tile * TILE, width)
            here = slice(head * HD, (head + 1) * HD)
            return dot(rows[:width, KEY], rows[span, here], NT), dot(rows[:width, VALUE], dt[here, span], NN)

        ahead = products(steps[0])
        for n, (head, tile) in enumerate(steps):
            scores, dprob = ahead
            if n + 1 < len(steps):
                ahead = products(steps[n + 1])
            here = slice(head * HD, (head + 1) * HD)
            width = (tile + 1) * TILE
            span = slice(tile * TILE, width)
            at = (head - first) * TOK
            spot = slice(at + tile * TILE, at + width)
            delta = jnp.sum(
                dt[here, span].astype(F32) * attn_ref[here, span].astype(F32), axis=0, keepdims=True
            )
            mask = keep_mask(tile, start)
            prob = jnp.exp2(jnp.where(mask, scores * EXP2_SCALE - stat_ref[head : head + 1, span], -jnp.inf))
            weight_t[:width, spot] = prob.astype(BF16)
            dscore = (prob * (dprob - delta)).astype(BF16)
            score_t[:width, spot] = dscore
            dq_t = dot(key_t[:, :width], dscore, NN) * SCALE
            dq[head, span, :] = dq_t.T.astype(BF16)
            if tile == TILES - 1:
                store = pltpu.make_async_copy(dq.at[head], dq_out.at[:, pl.ds(head * HD, HD)], dq_sems.at[head])
                store.start()
                stores.append(store)
        for tile in range(TILES):
            span = slice(tile * TILE, (tile + 1) * TILE)
            dk = jnp.zeros((TILE, HD), F32) if first == 0 else acc[span, :HD]
            dv = jnp.zeros((TILE, HD), F32) if first == 0 else acc[span, HD:]
            for head in range(first, first + PAIR):
                here = slice(head * HD, (head + 1) * HD)
                at = (head - first) * TOK
                spot = slice(at + tile * TILE, at + TOK)
                dk = dk + dot(score_t[span, spot], rows[tile * TILE :, here], NN)
                dv = dv + dot(weight_t[span, spot], dt[here, tile * TILE :], NT)
            if first + PAIR == HQ:
                kv_ref[span, :HD] = (dk * SCALE).astype(BF16)
                kv_ref[span, HD:] = dv.astype(BF16)
            else:
                acc[span, :HD] = dk
                acc[span, HD:] = dv
    for store in stores:
        store.wait()


def backward(rows, pack, d_attn_t, attn_t, stats, after):
    return pl.pallas_call(
        backward_kernel,
        out_shape=[shape((TOK, HQ * HD)), shape((TOK, 2 * HD)), TOKEN],
        in_specs=[VMEM] * 5 + [ANY],
        out_specs=[ANY, VMEM, VMEM],
        scratch_shapes=[
            pltpu.VMEM((HD, TOK), BF16),
            pltpu.VMEM((TOK, PAIR * TOK), BF16),
            pltpu.VMEM((TOK, PAIR * TOK), BF16),
            pltpu.VMEM((TOK, 2 * HD), F32),
            pltpu.VMEM((HQ, TOK, HD), BF16),
            pltpu.SemaphoreType.DMA((HQ,)),
        ],
        compiler_params=params(24),
        name="backward",
        cost_estimate=cost(30 * 10**9, 8 * 2**20, HQ * 655360),
    )(rows, pack, d_attn_t, attn_t, stats, after)


def add_pair_kernel(x_ref, keep_ref, got_hbm, *outs):
    *outs, token, got_ref, sems = outs
    for k in range(N_FSDP):
        pltpu.make_async_copy(got_hbm.at[k], got_ref.at[k], sems.at[k]).start()
    token[...] = jnp.zeros(token.shape, F32)
    x = x_ref[0]
    for k, out in enumerate(outs):
        shard = lax.rem(x + k, N_FSDP)
        pltpu.make_async_copy(got_hbm.at[shard], got_ref.at[shard], sems.at[shard]).wait()
        out[...] = (keep_ref[shard].astype(F32) + got_ref[shard].astype(F32)).astype(out.dtype)


def add_pair(x, keep, got):
    rows = keep.shape[0] // N_FSDP
    dims = (rows, HALF)
    return pl.pallas_call(
        add_pair_kernel,
        out_shape=[shape(dims, F32)] + [shape(dims)] * 3 + [TOKEN],
        in_specs=[SMEM, VMEM, ANY],
        out_specs=[VMEM] * 5,
        scratch_shapes=[pltpu.VMEM((N_FSDP, *dims), BF16), pltpu.SemaphoreType.DMA((N_FSDP,))],
        compiler_params=params(4),
        name="add_pair",
        cost_estimate=cost(4 * rows * HALF, 10 * rows * HALF * 2),
    )(x, keep.reshape(N_FSDP, *dims), got.reshape(N_FSDP, *dims))


def sum4(parts):
    total = parts[0].astype(F32)
    for part in parts[1:]:
        total = total + part.astype(F32)
    return total


def split_z_kernel(z_ref, _, *refs):
    parts, outs, total = refs[:4], refs[4:8], refs[8]
    total[...] = sum4([r[...] for r in parts])
    size = SHARD // 4
    z = z_ref[0]
    for k, out in enumerate(outs):
        at = pl.multiple_of(lax.rem(z + k, 4) * size, size)
        out[...] = total[pl.ds(at, size), :].astype(out.dtype)


def split_z(z, after, parts):
    dims = (SHARD // 4, HALF)
    return pl.pallas_call(
        split_z_kernel,
        out_shape=[shape(dims, F32)] + [shape(dims)] * 3,
        in_specs=[SMEM, ANY] + [VMEM] * 4,
        out_specs=[VMEM] * 4,
        scratch_shapes=[pltpu.VMEM((SHARD, HALF), F32)],
        compiler_params=params(4),
        name="split_z",
        cost_estimate=cost(4 * SHARD * HALF, 10 * SHARD * HALF),
    )(z, after, *parts)


def sum4_kernel(factor, *refs):
    refs[4][...] = (sum4([r[...] for r in refs[:4]]) * factor).astype(BF16)


def sum_four(parts, factor=1.0):
    return pl.pallas_call(
        functools.partial(sum4_kernel, factor),
        out_shape=shape(parts[0].shape),
        in_specs=[VMEM] * 4,
        out_specs=VMEM,
        compiler_params=params(8),
        name="sum_four",
        cost_estimate=cost(4 * parts[0].size, 10 * parts[0].size),
    )(*parts)


def join_z_kernel(z_ref, *refs):
    parts, out = refs[:4], refs[4]
    size = SHARD // 4
    for k, ref in enumerate(parts):
        at = pl.multiple_of(lax.rem(z_ref[0] - k + 4, 4) * size, size)
        out[pl.ds(at, size), :] = ref[...]


def join_z(z, parts):
    return pl.pallas_call(
        join_z_kernel,
        out_shape=shape((SHARD, HALF)),
        in_specs=[SMEM] + [VMEM] * 4,
        out_specs=VMEM,
        compiler_params=params(4),
        name="join_z",
        cost_estimate=cost(0, 4 * SHARD * HALF),
    )(z, *parts)


def lay_out_kernel(core_ref, own, got, out):
    for part, side in ((own, core_ref[0]), (got, 1 - core_ref[0])):
        columns = pl.ds(pl.multiple_of(side * HALF, HALF), HALF)
        out[:, columns] = part[...].astype(F32)


def lay_out(core, own, got):
    return pl.pallas_call(
        lay_out_kernel,
        out_shape=shape((SHARD, D), F32),
        in_specs=[SMEM, VMEM, VMEM],
        out_specs=VMEM,
        compiler_params=params(4),
        name="lay_out",
        cost_estimate=cost(SHARD * D, 6 * SHARD * D),
    )(core, own, got)


def dp_shift(dy, dz, dc):
    pairs = []
    for i in range(32):
        y, z, c = i // 8, (i // 2) % 4, i % 2
        pairs.append((i, ((y + dy) % 4) * 8 + ((z + dz) % 4) * 2 + (c + dc) % 2))
    return pairs


def x_shift(k):
    return [(i, (i + k) % N_FSDP) for i in range(N_FSDP)]


def per_device(stash, stash_place, pack_start, d_out, out_weight):
    group = lax.axis_index("dp")
    x = lax.axis_index("fsdp")
    core = lax.rem(group, 2)
    z = lax.rem(group // 2, 4)
    held = stash.reshape(NB, BLK, WIDTH)
    peers = jnp.arange(NB, dtype=jnp.int32)
    holder = stash_place // NB
    slot = stash_place % NB
    chosen = jnp.sum(jnp.where((holder == group) & (peers[:, None] != group), slot, 0), axis=1)
    x1, z1, core1 = x.reshape(1), z.reshape(1), core.reshape(1)

    incoming = lax.all_to_all(held[chosen], "dp", split_axis=0, concat_axis=0, tiled=True)
    swap = dp_shift(0, 0, 1)
    half = lax.dynamic_slice_in_dim(out_weight, core * HALF, HALF, 1)
    weight_mine = [lax.ppermute(half, "fsdp", x_shift(k)) for k in (1, 2, 3)]
    weight_other = [lax.ppermute(part, "dp", swap) for part in weight_mine]
    d_attn_t = d_attn_transposed(x1, core1, out_weight, weight_mine, weight_other, d_out)

    pack = pack_start.reshape(1, TOK)
    rows, attn_t, stats, send = forward(group.reshape(1), stash_place, held, incoming, pack, d_out, d_attn_t)
    keep = keep_half(core1, attn_t, d_out)
    *parts, x_token = add_pair(x1, keep, lax.ppermute(send, "dp", swap))
    by_x = [parts[0]] + [lax.ppermute(parts[k], "fsdp", x_shift(k)) for k in (2, 1, 3)]
    grad_query, grad_keyval, token = backward(rows, pack, d_attn_t, attn_t, stats, x_token)
    by_z = split_z(z1, token, by_x)
    by_z = [by_z[0]] + [lax.ppermute(by_z[k], "dp", dp_shift(0, k, 0)) for k in (2, 1, 3)]
    z_sum = sum_four(by_z)
    by_y = [z_sum] + [lax.ppermute(z_sum, "dp", dp_shift(k, 0, 0)) for k in (1, 3, 2)]
    factor = (TOK * lax.axis_size("dp") * lax.axis_size("fsdp")) ** (-0.5)
    total = sum_four(by_y, factor)
    by_z = {k: lax.ppermute(total, "dp", dp_shift(0, k, 0)) for k in (1, 3, 2)}
    own = join_z(z1, [total] + [by_z[k] for k in (1, 2, 3)])
    grad_weight = lay_out(core1, own, lax.ppermute(own, "dp", swap))
    return (grad_query, grad_keyval, grad_weight)


def solution(mesh):
    in_specs = (
        P("dp", "fsdp", None, None, None),
        P(),
        P(("dp", "fsdp")),
        P(("dp", "fsdp"), None),
        P("fsdp", None),
    )
    out_specs = (P(("dp", "fsdp"), None), P(("dp", "fsdp"), None), P("fsdp", None))
    return jax.shard_map(
        per_device, mesh=mesh, in_specs=in_specs, out_specs=out_specs, check_vma=False
    )
```

```python
import functools

import jax
import jax.numpy as jnp
from jax import lax
from jax.experimental import pallas as pl
from jax.experimental.pallas import tpu as pltpu
from jax.sharding import PartitionSpec as P

HQ = 6
HD = 128
TILE = 256
TOK = 1024
TILES = TOK // TILE
D = 1536
HALF = D // 2
NB = 32
BLK = 32
WIDTH = 1024
N_FSDP = 4
SHARD = HQ * HD // N_FSDP
SCALE = HD ** (-0.5)
EXP2_SCALE = SCALE * 1.4426950408889634
KEY = slice(HQ * HD, (HQ + 1) * HD)
VALUE = slice((HQ + 1) * HD, (HQ + 2) * HD)
NT = (((1,), (1,)), ((), ()))
NN = (((1,), (0,)), ((), ()))
ANY = pl.BlockSpec(memory_space=pl.ANY)
SMEM = pl.BlockSpec(memory_space=pltpu.SMEM)
VMEM = pl.BlockSpec(memory_space=pltpu.VMEM)
HBM = pl.BlockSpec(memory_space=pltpu.HBM)


def params(mib):
    return pltpu.CompilerParams(vmem_limit_bytes=mib * 2**20)


BF16 = jnp.bfloat16
LARGE = 56
F32 = jnp.float32


def dot(a, b, dims):
    return lax.dot_general(a, b, dims, preferred_element_type=F32)


def shape(dims, dtype=BF16):
    return jax.ShapeDtypeStruct(dims, dtype)


TOKEN = shape((8, 128), F32)


def cost(flops, size, exps=0):
    return pl.CostEstimate(flops=int(flops), bytes_accessed=int(size), transcendentals=int(exps))


def d_attn_kernel(x_ref, core_ref, *refs):
    own, mine, others, dout, out_ref, weight, sems = (
        refs[0], refs[1:4], refs[4:7], *refs[7:]
    )
    x, core = x_ref[0], core_ref[0]

    def shard_rows(k):
        return pl.ds(pl.multiple_of(lax.rem(x - k + N_FSDP, N_FSDP) * SHARD, SHARD), SHARD)

    loads = [pltpu.make_async_copy(own, weight.at[shard_rows(0), :], sems.at[0])]
    for k in range(1, N_FSDP):
        for i, (part, side) in enumerate(((mine[k - 1], core), (others[k - 1], 1 - core))):
            columns = pl.ds(pl.multiple_of(side * HALF, HALF), HALF)
            loads.append(pltpu.make_async_copy(part, weight.at[shard_rows(k), columns], sems.at[2 * k - 1 + i]))
    for load in loads:
        load.start()
    for load in loads:
        load.wait()
    out_ref[...] = dot(weight[...], dout[...], NT).astype(BF16)


def d_attn_transposed(x, core, own, mine, others, dout):
    return pl.pallas_call(
        d_attn_kernel,
        out_shape=shape((HQ * HD, TOK)),
        in_specs=[SMEM, SMEM] + [ANY] * 7 + [VMEM],
        out_specs=VMEM,
        scratch_shapes=[pltpu.VMEM((HQ * HD, D), BF16), pltpu.SemaphoreType.DMA((7,))],
        compiler_params=params(10),
        name="d_attn",
        cost_estimate=cost(2 * TOK * D * HQ * HD, 8 * 2**20),
    )(x, core, own, *mine, *others, dout)


TRIO = 3


def keep_mask(tile, start):
    width = (tile + 1) * TILE
    key = lax.broadcasted_iota(jnp.int32, (width, TILE), 0)
    query = tile * TILE + lax.broadcasted_iota(jnp.int32, (width, TILE), 1)
    return (key >= start[:, tile * TILE : width]) & (key <= query)


def transposed(x):
    return x.astype(F32).T.astype(BF16)


def gather_rows(group, place_ref, held_ref, inc_ref, rows, sems):
    def copy(ref, b, source):
        return pltpu.make_async_copy(ref.at[source], rows.at[pl.ds(b * BLK, BLK), :], sems.at[b])

    for b in range(NB):
        place = place_ref[group, b]
        holder = lax.shift_right_logical(place, 5)
        slot = place - holder * NB

        @pl.when(holder == group)
        def _(b=b, slot=slot):
            copy(held_ref, b, slot).start()

        @pl.when(holder != group)
        def _(b=b, holder=holder):
            copy(inc_ref, b, holder).start()

    def wait_rows(tile):
        per_tile = TILE // BLK
        for b in range(tile * per_tile, (tile + 1) * per_tile):
            copy(held_ref, b, 0).wait()

    return wait_rows


def forward_kernel(
    group_ref, place_ref, held_ref, inc_ref, pack_ref, dout_hbm, _,
    rows_out, attn_out, stat_ref, send_out,
    rows, attn_ref, send_ref, dout, value_t, sems, side_sems, attn_sems,
):
    group = group_ref[0]
    wait_rows = gather_rows(group, place_ref, held_ref, inc_ref, rows, sems)
    other = pl.ds(pl.multiple_of((1 - lax.rem(group, 2)) * HALF, HALF), HALF)
    dout_copy = pltpu.make_async_copy(dout_hbm.at[:, other], dout, side_sems.at[0])
    dout_copy.start()
    rows_copy = pltpu.make_async_copy(rows, rows_out, side_sems.at[1])
    send_copies = [
        pltpu.make_async_copy(
            send_ref.at[pl.ds(half * (HQ * HD // 2), HQ * HD // 2), :],
            send_out.at[pl.ds(half * (HQ * HD // 2), HQ * HD // 2), :],
            side_sems.at[2 + half],
        )
        for half in range(2)
    ]
    attn_copies = [
        pltpu.make_async_copy(
            attn_ref.at[pl.ds(h * HD, HD), :], attn_out.at[pl.ds(h * HD, HD), :], attn_sems.at[h]
        )
        for h in range(HQ)
    ]
    start = pack_ref[...]
    for tile in range(TILES):
        width = (tile + 1) * TILE
        span = slice(tile * TILE, width)
        wait_rows(tile)
        if tile == TILES - 1:
            rows_copy.start()
        value_t[:, span] = transposed(rows[span, VALUE])
        masks = jnp.concatenate([keep_mask(tile, start)] * TRIO, axis=1)

        def raw_scores(first, width=width, span=span):
            query = jnp.concatenate(
                [rows[span, h * HD : (h + 1) * HD] for h in range(first, first + TRIO)], axis=0
            )
            return dot(rows[:width, KEY], query, NT)

        ahead = raw_scores(0)
        for first in range(0, HQ, TRIO):
            scores = ahead
            if first + TRIO < HQ:
                ahead = raw_scores(first + TRIO)
            scores = jnp.where(masks, scores, -jnp.inf)
            top = jnp.max(scores, axis=0, keepdims=True)
            expo = jnp.exp2((scores - top) * EXP2_SCALE)
            total = jnp.sum(expo, axis=0, keepdims=True)
            attn = (dot(value_t[:, :width], expo.astype(BF16), NN) * (1.0 / total)).astype(BF16)
            stat = top * EXP2_SCALE + jnp.log2(total)
            for k in range(TRIO):
                part = slice(k * TILE, (k + 1) * TILE)
                attn_ref[(first + k) * HD : (first + k + 1) * HD, span] = attn[:, part]
                stat_ref[first + k : first + k + 1, span] = stat[:, part]
    for copy in attn_copies:
        copy.start()
    dout_copy.wait()
    for half, copy in enumerate(send_copies):
        part = slice(half * (HQ * HD // 2), (half + 1) * (HQ * HD // 2))
        send_ref[part, :] = dot(attn_ref[part, :], dout[...], NN).astype(BF16)
        copy.start()
    for copy in (rows_copy, *attn_copies, *send_copies):
        copy.wait()


def forward(group, place, held, inc, pack, dout, after):
    n = HQ * HD
    return pl.pallas_call(
        forward_kernel,
        out_shape=[
            shape((TOK, WIDTH)), shape((n, TOK)), shape((8, TOK), F32), shape((n, HALF))
        ],
        in_specs=[SMEM, SMEM, ANY, ANY, VMEM, ANY, ANY],
        out_specs=[ANY, ANY, VMEM, ANY],
        scratch_shapes=[
            pltpu.VMEM((TOK, WIDTH), BF16),
            pltpu.VMEM((n, TOK), BF16),
            pltpu.VMEM((n, HALF), BF16),
            pltpu.VMEM((TOK, HALF), BF16),
            pltpu.VMEM((HD, TOK), BF16),
            pltpu.SemaphoreType.DMA((NB,)),
            pltpu.SemaphoreType.DMA((4,)),
            pltpu.SemaphoreType.DMA((HQ,)),
        ],
        compiler_params=params(LARGE),
        name="forward",
        cost_estimate=cost(12 * 10**9, 8 * 2**20, HQ * 655360),
    )(group, place, held, inc, pack, dout, after)


def keep_kernel(core_ref, attn_ref, dout_hbm, keep_ref, dout, sem):
    mine = pl.ds(pl.multiple_of(core_ref[0] * HALF, HALF), HALF)
    load = pltpu.make_async_copy(dout_hbm.at[:, mine], dout, sem)
    load.start()
    load.wait()
    keep_ref[...] = dot(attn_ref[...], dout[...], NN).astype(BF16)


def keep_half(core, attn_t, dout):
    return pl.pallas_call(
        keep_kernel,
        out_shape=shape((HQ * HD, HALF)),
        in_specs=[SMEM, VMEM, ANY],
        out_specs=VMEM,
        scratch_shapes=[pltpu.VMEM((TOK, HALF), BF16), pltpu.SemaphoreType.DMA],
        compiler_params=params(12),
        name="keep_half",
        cost_estimate=cost(2 * TOK * HALF * HQ * HD, 8 * 2**20),
    )(core, attn_t, dout)


PAIR = 2


def backward_kernel(
    rows, pack_ref, dt, attn_ref, stat_ref, _, dq_out, kv_ref, token,
    key_t, weight_t, score_t, acc, dq, dq_sems,
):
    token[...] = jnp.zeros(token.shape, F32)
    start = pack_ref[...]
    key_t[...] = transposed(rows[:, KEY])
    stores = []
    for first in range(0, HQ, PAIR):
        heads = range(first, first + PAIR)
        steps = [(head, tile) for head in heads for tile in range(TILES)]

        def products(step):
            head, tile = step
            width = (tile + 1) * TILE
            span = slice(tile * TILE, width)
            here = slice(head * HD, (head + 1) * HD)
            return dot(rows[:width, KEY], rows[span, here], NT), dot(rows[:width, VALUE], dt[here, span], NN)

        ahead = products(steps[0])
        for n, (head, tile) in enumerate(steps):
            scores, dprob = ahead
            if n + 1 < len(steps):
                ahead = products(steps[n + 1])
            here = slice(head * HD, (head + 1) * HD)
            width = (tile + 1) * TILE
            span = slice(tile * TILE, width)
            at = (head - first) * TOK
            spot = slice(at + tile * TILE, at + width)
            delta = jnp.sum(
                dt[here, span].astype(F32) * attn_ref[here, span].astype(F32), axis=0, keepdims=True
            )
            mask = keep_mask(tile, start)
            prob = jnp.exp2(jnp.where(mask, scores * EXP2_SCALE - stat_ref[head : head + 1, span], -jnp.inf))
            weight_t[:width, spot] = prob.astype(BF16)
            dscore = (prob * (dprob - delta)).astype(BF16)
            score_t[:width, spot] = dscore
            dq_t = dot(key_t[:, :width], dscore, NN) * SCALE
            dq[head, span, :] = dq_t.T.astype(BF16)
            if tile == TILES - 1:
                store = pltpu.make_async_copy(dq.at[head], dq_out.at[:, pl.ds(head * HD, HD)], dq_sems.at[head])
                store.start()
                stores.append(store)
        for tile in range(TILES):
            span = slice(tile * TILE, (tile + 1) * TILE)
            dk = jnp.zeros((TILE, HD), F32) if first == 0 else acc[span, :HD]
            dv = jnp.zeros((TILE, HD), F32) if first == 0 else acc[span, HD:]
            for head in range(first, first + PAIR):
                here = slice(head * HD, (head + 1) * HD)
                at = (head - first) * TOK
                spot = slice(at + tile * TILE, at + TOK)
                dk = dk + dot(score_t[span, spot], rows[tile * TILE :, here], NN)
                dv = dv + dot(weight_t[span, spot], dt[here, tile * TILE :], NT)
            if first + PAIR == HQ:
                kv_ref[span, :HD] = (dk * SCALE).astype(BF16)
                kv_ref[span, HD:] = dv.astype(BF16)
            else:
                acc[span, :HD] = dk
                acc[span, HD:] = dv
    for store in stores:
        store.wait()


def backward(rows, pack, d_attn_t, attn_t, stats, after):
    return pl.pallas_call(
        backward_kernel,
        out_shape=[shape((TOK, HQ * HD)), shape((TOK, 2 * HD)), TOKEN],
        in_specs=[VMEM] * 5 + [ANY],
        out_specs=[ANY, VMEM, VMEM],
        scratch_shapes=[
            pltpu.VMEM((HD, TOK), BF16),
            pltpu.VMEM((TOK, PAIR * TOK), BF16),
            pltpu.VMEM((TOK, PAIR * TOK), BF16),
            pltpu.VMEM((TOK, 2 * HD), F32),
            pltpu.VMEM((HQ, TOK, HD), BF16),
            pltpu.SemaphoreType.DMA((HQ,)),
        ],
        compiler_params=params(24),
        name="backward",
        cost_estimate=cost(30 * 10**9, 8 * 2**20, HQ * 655360),
    )(rows, pack, d_attn_t, attn_t, stats, after)


def add_pair_kernel(x_ref, keep_ref, got_hbm, *outs):
    *outs, token, got_ref, sems = outs
    for k in range(N_FSDP):
        pltpu.make_async_copy(got_hbm.at[k], got_ref.at[k], sems.at[k]).start()
    token[...] = jnp.zeros(token.shape, F32)
    x = x_ref[0]
    for k, out in enumerate(outs):
        shard = lax.rem(x + k, N_FSDP)
        pltpu.make_async_copy(got_hbm.at[shard], got_ref.at[shard], sems.at[shard]).wait()
        out[...] = (keep_ref[shard].astype(F32) + got_ref[shard].astype(F32)).astype(out.dtype)


def add_pair(x, keep, got):
    rows = keep.shape[0] // N_FSDP
    dims = (rows, HALF)
    return pl.pallas_call(
        add_pair_kernel,
        out_shape=[shape(dims, F32)] + [shape(dims)] * 3 + [TOKEN],
        in_specs=[SMEM, VMEM, ANY],
        out_specs=[VMEM] * 5,
        scratch_shapes=[pltpu.VMEM((N_FSDP, *dims), BF16), pltpu.SemaphoreType.DMA((N_FSDP,))],
        compiler_params=params(4),
        name="add_pair",
        cost_estimate=cost(4 * rows * HALF, 10 * rows * HALF * 2),
    )(x, keep.reshape(N_FSDP, *dims), got.reshape(N_FSDP, *dims))


def sum4(parts):
    own, next_one, last, opposite = (part.astype(F32) for part in parts)
    return (own + opposite) + (next_one + last)


def split_z_kernel(z_ref, _, *refs):
    parts, outs, total = refs[:4], refs[4:8], refs[8]
    total[...] = sum4([r[...] for r in parts])
    size = SHARD // 4
    z = z_ref[0]
    for k, out in enumerate(outs):
        at = pl.multiple_of(lax.rem(z + k, 4) * size, size)
        out[...] = total[pl.ds(at, size), :].astype(out.dtype)


def split_z(z, after, parts):
    dims = (SHARD // 4, HALF)
    return pl.pallas_call(
        split_z_kernel,
        out_shape=[shape(dims, F32)] + [shape(dims)] * 3,
        in_specs=[SMEM, ANY] + [VMEM] * 4,
        out_specs=[VMEM] * 4,
        scratch_shapes=[pltpu.VMEM((SHARD, HALF), F32)],
        compiler_params=params(4),
        name="split_z",
        cost_estimate=cost(4 * SHARD * HALF, 10 * SHARD * HALF),
    )(z, after, *parts)


def sum4_kernel(factor, *refs):
    refs[4][...] = (sum4([r[...] for r in refs[:4]]) * factor).astype(BF16)


def sum_four(parts, factor=1.0):
    return pl.pallas_call(
        functools.partial(sum4_kernel, factor),
        out_shape=shape(parts[0].shape),
        in_specs=[VMEM] * 4,
        out_specs=VMEM,
        compiler_params=params(8),
        name="sum_four",
        cost_estimate=cost(4 * parts[0].size, 10 * parts[0].size),
    )(*parts)


def join_z_kernel(z_ref, *refs):
    parts, out = refs[:4], refs[4]
    size = SHARD // 4
    for k, ref in enumerate(parts):
        at = pl.multiple_of(lax.rem(z_ref[0] - k + 4, 4) * size, size)
        out[pl.ds(at, size), :] = ref[...]


def join_z(z, parts):
    return pl.pallas_call(
        join_z_kernel,
        out_shape=shape((SHARD, HALF)),
        in_specs=[SMEM] + [VMEM] * 4,
        out_specs=VMEM,
        compiler_params=params(4),
        name="join_z",
        cost_estimate=cost(0, 4 * SHARD * HALF),
    )(z, *parts)


def lay_out_kernel(core_ref, own, got, out):
    for part, side in ((own, core_ref[0]), (got, 1 - core_ref[0])):
        columns = pl.ds(pl.multiple_of(side * HALF, HALF), HALF)
        out[:, columns] = part[...].astype(F32)


def lay_out(core, own, got):
    return pl.pallas_call(
        lay_out_kernel,
        out_shape=shape((SHARD, D), F32),
        in_specs=[SMEM, VMEM, VMEM],
        out_specs=VMEM,
        compiler_params=params(4),
        name="lay_out",
        cost_estimate=cost(SHARD * D, 6 * SHARD * D),
    )(core, own, got)


def dp_shift(dy, dz, dc):
    pairs = []
    for i in range(32):
        y, z, c = i // 8, (i // 2) % 4, i % 2
        pairs.append((i, ((y + dy) % 4) * 8 + ((z + dz) % 4) * 2 + (c + dc) % 2))
    return pairs


def x_shift(k):
    return [(i, (i + k) % N_FSDP) for i in range(N_FSDP)]


def per_device(stash, stash_place, pack_start, d_out, out_weight):
    group = lax.axis_index("dp")
    x = lax.axis_index("fsdp")
    core = lax.rem(group, 2)
    z = lax.rem(group // 2, 4)
    held = stash.reshape(NB, BLK, WIDTH)
    peers = jnp.arange(NB, dtype=jnp.int32)
    holder = stash_place // NB
    slot = stash_place % NB
    chosen = jnp.sum(jnp.where((holder == group) & (peers[:, None] != group), slot, 0), axis=1)
    x1, z1, core1 = x.reshape(1), z.reshape(1), core.reshape(1)

    incoming = lax.all_to_all(held[chosen], "dp", split_axis=0, concat_axis=0, tiled=True)
    swap = dp_shift(0, 0, 1)
    half = lax.dynamic_slice_in_dim(out_weight, core * HALF, HALF, 1)
    weight_mine = [lax.ppermute(half, "fsdp", x_shift(k)) for k in (1, 2, 3)]
    weight_other = [lax.ppermute(part, "dp", swap) for part in weight_mine]
    d_attn_t = d_attn_transposed(x1, core1, out_weight, weight_mine, weight_other, d_out)

    pack = pack_start.reshape(1, TOK)
    rows, attn_t, stats, send = forward(group.reshape(1), stash_place, held, incoming, pack, d_out, d_attn_t)
    keep = keep_half(core1, attn_t, d_out)
    *parts, x_token = add_pair(x1, keep, lax.ppermute(send, "dp", swap))
    by_x = [parts[0]] + [lax.ppermute(parts[k], "fsdp", x_shift(k)) for k in (2, 1, 3)]
    grad_query, grad_keyval, token = backward(rows, pack, d_attn_t, attn_t, stats, x_token)
    by_z = split_z(z1, token, by_x)
    by_z = [by_z[0]] + [lax.ppermute(by_z[k], "dp", dp_shift(0, k, 0)) for k in (2, 1, 3)]
    z_sum = sum_four(by_z)
    by_y = [z_sum] + [lax.ppermute(z_sum, "dp", dp_shift(k, 0, 0)) for k in (1, 3, 2)]
    factor = (TOK * lax.axis_size("dp") * lax.axis_size("fsdp")) ** (-0.5)
    total = sum_four(by_y, factor)
    by_z = {k: lax.ppermute(total, "dp", dp_shift(0, k, 0)) for k in (1, 3, 2)}
    own = join_z(z1, [total] + [by_z[k] for k in (1, 2, 3)])
    grad_weight = lay_out(core1, own, lax.ppermute(own, "dp", swap))
    return (grad_query, grad_keyval, grad_weight)


def solution(mesh):
    in_specs = (
        P("dp", "fsdp", None, None, None),
        P(),
        P(("dp", "fsdp")),
        P(("dp", "fsdp"), None),
        P("fsdp", None),
    )
    out_specs = (P(("dp", "fsdp"), None), P(("dp", "fsdp"), None), P("fsdp", None))
    return jax.shard_map(
        per_device, mesh=mesh, in_specs=in_specs, out_specs=out_specs, check_vma=False
    )
```

```python
import functools

import jax
import jax.numpy as jnp
from jax import lax
from jax.experimental import pallas as pl
from jax.experimental.pallas import tpu as pltpu
from jax.sharding import PartitionSpec as P

HQ = 6
HD = 128
TILE = 256
TOK = 1024
TILES = TOK // TILE
D = 1536
HALF = D // 2
NB = 32
BLK = 32
WIDTH = 1024
N_FSDP = 4
SHARD = HQ * HD // N_FSDP
SCALE = HD ** (-0.5)
EXP2_SCALE = SCALE * 1.4426950408889634
KEY = slice(HQ * HD, (HQ + 1) * HD)
VALUE = slice((HQ + 1) * HD, (HQ + 2) * HD)
NT = (((1,), (1,)), ((), ()))
NN = (((1,), (0,)), ((), ()))
ANY = pl.BlockSpec(memory_space=pl.ANY)
SMEM = pl.BlockSpec(memory_space=pltpu.SMEM)
VMEM = pl.BlockSpec(memory_space=pltpu.VMEM)
HBM = pl.BlockSpec(memory_space=pltpu.HBM)


def params(mib):
    return pltpu.CompilerParams(vmem_limit_bytes=mib * 2**20)


BF16 = jnp.bfloat16
LARGE = 56
F32 = jnp.float32


def dot(a, b, dims):
    return lax.dot_general(a, b, dims, preferred_element_type=F32)


def shape(dims, dtype=BF16):
    return jax.ShapeDtypeStruct(dims, dtype)


TOKEN = shape((8, 128), F32)


def cost(flops, size, exps=0):
    return pl.CostEstimate(flops=int(flops), bytes_accessed=int(size), transcendentals=int(exps))


def d_attn_kernel(x_ref, core_ref, *refs):
    own, mine, others, dout, out_ref, weight, sems = (
        refs[0], refs[1:4], refs[4:7], *refs[7:]
    )
    x, core = x_ref[0], core_ref[0]

    def shard_rows(k):
        return pl.ds(pl.multiple_of(lax.rem(x - k + N_FSDP, N_FSDP) * SHARD, SHARD), SHARD)

    loads = [pltpu.make_async_copy(own, weight.at[shard_rows(0), :], sems.at[0])]
    for k in range(1, N_FSDP):
        for i, (part, side) in enumerate(((mine[k - 1], core), (others[k - 1], 1 - core))):
            columns = pl.ds(pl.multiple_of(side * HALF, HALF), HALF)
            loads.append(pltpu.make_async_copy(part, weight.at[shard_rows(k), columns], sems.at[2 * k - 1 + i]))
    for load in loads:
        load.start()
    for load in loads:
        load.wait()
    out_ref[...] = dot(weight[...], dout[...], NT).astype(BF16)


def d_attn_transposed(x, core, own, mine, others, dout):
    return pl.pallas_call(
        d_attn_kernel,
        out_shape=shape((HQ * HD, TOK)),
        in_specs=[SMEM, SMEM] + [ANY] * 7 + [VMEM],
        out_specs=VMEM,
        scratch_shapes=[pltpu.VMEM((HQ * HD, D), BF16), pltpu.SemaphoreType.DMA((7,))],
        compiler_params=params(10),
        name="d_attn",
        cost_estimate=cost(2 * TOK * D * HQ * HD, 8 * 2**20),
    )(x, core, own, *mine, *others, dout)


TRIO = 3


def keep_mask(tile, start):
    width = (tile + 1) * TILE
    key = lax.broadcasted_iota(jnp.int32, (width, TILE), 0)
    query = tile * TILE + lax.broadcasted_iota(jnp.int32, (width, TILE), 1)
    return (key >= start[:, tile * TILE : width]) & (key <= query)


def transposed(x):
    return x.astype(F32).T.astype(BF16)


def gather_rows(group, place_ref, held_ref, inc_ref, rows, sems):
    def copy(ref, b, source):
        return pltpu.make_async_copy(ref.at[source], rows.at[pl.ds(b * BLK, BLK), :], sems.at[b])

    for b in range(NB):
        place = place_ref[group, b]
        holder = lax.shift_right_logical(place, 5)
        slot = place - holder * NB

        @pl.when(holder == group)
        def _(b=b, slot=slot):
            copy(held_ref, b, slot).start()

        @pl.when(holder != group)
        def _(b=b, holder=holder):
            copy(inc_ref, b, holder).start()

    def wait_rows(tile):
        per_tile = TILE // BLK
        for b in range(tile * per_tile, (tile + 1) * per_tile):
            copy(held_ref, b, 0).wait()

    return wait_rows


def forward_kernel(
    group_ref, place_ref, held_ref, inc_ref, pack_ref, dout_hbm, _,
    rows_out, attn_out, stat_ref, send_out,
    rows, attn_ref, send_ref, dout, value_t, sems, side_sems, attn_sems,
):
    group = group_ref[0]
    wait_rows = gather_rows(group, place_ref, held_ref, inc_ref, rows, sems)
    other = pl.ds(pl.multiple_of((1 - lax.rem(group, 2)) * HALF, HALF), HALF)
    dout_copy = pltpu.make_async_copy(dout_hbm.at[:, other], dout, side_sems.at[0])
    dout_copy.start()
    rows_copy = pltpu.make_async_copy(rows, rows_out, side_sems.at[1])
    send_copies = [
        pltpu.make_async_copy(
            send_ref.at[pl.ds(half * (HQ * HD // 2), HQ * HD // 2), :],
            send_out.at[pl.ds(half * (HQ * HD // 2), HQ * HD // 2), :],
            side_sems.at[2 + half],
        )
        for half in range(2)
    ]
    attn_copies = [
        pltpu.make_async_copy(
            attn_ref.at[pl.ds(h * HD, HD), :], attn_out.at[pl.ds(h * HD, HD), :], attn_sems.at[h]
        )
        for h in range(HQ)
    ]
    start = pack_ref[...]
    for tile in range(TILES):
        width = (tile + 1) * TILE
        span = slice(tile * TILE, width)
        wait_rows(tile)
        if tile == TILES - 1:
            rows_copy.start()
        value_t[:, span] = transposed(rows[span, VALUE])
        masks = jnp.concatenate([keep_mask(tile, start)] * TRIO, axis=1)

        def raw_scores(first, width=width, span=span):
            query = jnp.concatenate(
                [rows[span, h * HD : (h + 1) * HD] for h in range(first, first + TRIO)], axis=0
            )
            return dot(rows[:width, KEY], query, NT)

        ahead = raw_scores(0)
        for first in range(0, HQ, TRIO):
            scores = ahead
            if first + TRIO < HQ:
                ahead = raw_scores(first + TRIO)
            scores = jnp.where(masks, scores, -jnp.inf)
            top = jnp.max(scores, axis=0, keepdims=True)
            expo = jnp.exp2((scores - top) * EXP2_SCALE)
            total = jnp.sum(expo, axis=0, keepdims=True)
            attn = (dot(value_t[:, :width], expo.astype(BF16), NN) * (1.0 / total)).astype(BF16)
            stat = top * EXP2_SCALE + jnp.log2(total)
            for k in range(TRIO):
                part = slice(k * TILE, (k + 1) * TILE)
                attn_ref[(first + k) * HD : (first + k + 1) * HD, span] = attn[:, part]
                stat_ref[first + k : first + k + 1, span] = stat[:, part]
    for copy in attn_copies:
        copy.start()
    dout_copy.wait()
    for half, copy in enumerate(send_copies):
        part = slice(half * (HQ * HD // 2), (half + 1) * (HQ * HD // 2))
        send_ref[part, :] = dot(attn_ref[part, :], dout[...], NN).astype(BF16)
        copy.start()
    for copy in (rows_copy, *attn_copies, *send_copies):
        copy.wait()


def forward(group, place, held, inc, pack, dout, after):
    n = HQ * HD
    return pl.pallas_call(
        forward_kernel,
        out_shape=[
            shape((TOK, WIDTH)), shape((n, TOK)), shape((8, TOK), F32), shape((n, HALF))
        ],
        in_specs=[SMEM, SMEM, ANY, ANY, VMEM, ANY, ANY],
        out_specs=[ANY, ANY, VMEM, ANY],
        scratch_shapes=[
            pltpu.VMEM((TOK, WIDTH), BF16),
            pltpu.VMEM((n, TOK), BF16),
            pltpu.VMEM((n, HALF), BF16),
            pltpu.VMEM((TOK, HALF), BF16),
            pltpu.VMEM((HD, TOK), BF16),
            pltpu.SemaphoreType.DMA((NB,)),
            pltpu.SemaphoreType.DMA((4,)),
            pltpu.SemaphoreType.DMA((HQ,)),
        ],
        compiler_params=params(LARGE),
        name="forward",
        cost_estimate=cost(12 * 10**9, 8 * 2**20, HQ * 655360),
    )(group, place, held, inc, pack, dout, after)


def keep_kernel(core_ref, attn_ref, dout_hbm, keep_ref, dout, sem):
    mine = pl.ds(pl.multiple_of(core_ref[0] * HALF, HALF), HALF)
    load = pltpu.make_async_copy(dout_hbm.at[:, mine], dout, sem)
    load.start()
    load.wait()
    keep_ref[...] = dot(attn_ref[...], dout[...], NN).astype(BF16)


def keep_half(core, attn_t, dout):
    return pl.pallas_call(
        keep_kernel,
        out_shape=shape((HQ * HD, HALF)),
        in_specs=[SMEM, VMEM, ANY],
        out_specs=VMEM,
        scratch_shapes=[pltpu.VMEM((TOK, HALF), BF16), pltpu.SemaphoreType.DMA],
        compiler_params=params(12),
        name="keep_half",
        cost_estimate=cost(2 * TOK * HALF * HQ * HD, 8 * 2**20),
    )(core, attn_t, dout)


PAIR = 2


def backward_kernel(
    rows, pack_ref, dt, attn_ref, stat_ref, _, dq_out, kv_ref, token,
    key_t, weight_t, score_t, acc, dq, dq_sems,
):
    token[...] = jnp.zeros(token.shape, F32)
    start = pack_ref[...]
    key_t[...] = transposed(rows[:, KEY])
    stores = []
    for first in range(0, HQ, PAIR):
        heads = range(first, first + PAIR)
        steps = [(head, tile) for head in heads for tile in range(TILES)]

        def products(step):
            head, tile = step
            width = (tile + 1) * TILE
            span = slice(tile * TILE, width)
            here = slice(head * HD, (head + 1) * HD)
            return dot(rows[:width, KEY], rows[span, here], NT), dot(rows[:width, VALUE], dt[here, span], NN)

        ahead = products(steps[0])
        for n, (head, tile) in enumerate(steps):
            scores, dprob = ahead
            if n + 1 < len(steps):
                ahead = products(steps[n + 1])
            here = slice(head * HD, (head + 1) * HD)
            width = (tile + 1) * TILE
            span = slice(tile * TILE, width)
            at = (head - first) * TOK
            spot = slice(at + tile * TILE, at + width)
            delta = jnp.sum(
                dt[here, span].astype(F32) * attn_ref[here, span].astype(F32), axis=0, keepdims=True
            )
            mask = keep_mask(tile, start)
            prob = jnp.exp2(jnp.where(mask, scores * EXP2_SCALE - stat_ref[head : head + 1, span], -jnp.inf))
            weight_t[:width, spot] = prob.astype(BF16)
            dscore = (prob * (dprob - delta)).astype(BF16)
            score_t[:width, spot] = dscore
            dq_t = dot(key_t[:, :width], dscore, NN) * SCALE
            dq[head, span, :] = dq_t.T.astype(BF16)
            if tile == TILES - 1:
                store = pltpu.make_async_copy(dq.at[head], dq_out.at[:, pl.ds(head * HD, HD)], dq_sems.at[head])
                store.start()
                stores.append(store)
        for tile in range(TILES):
            span = slice(tile * TILE, (tile + 1) * TILE)
            dk = jnp.zeros((TILE, HD), F32) if first == 0 else acc[span, :HD]
            dv = jnp.zeros((TILE, HD), F32) if first == 0 else acc[span, HD:]
            for head in range(first, first + PAIR):
                here = slice(head * HD, (head + 1) * HD)
                at = (head - first) * TOK
                spot = slice(at + tile * TILE, at + TOK)
                dk = dk + dot(score_t[span, spot], rows[tile * TILE :, here], NN)
                dv = dv + dot(weight_t[span, spot], dt[here, tile * TILE :], NT)
            if first + PAIR == HQ:
                kv_ref[span, :HD] = (dk * SCALE).astype(BF16)
                kv_ref[span, HD:] = dv.astype(BF16)
            else:
                acc[span, :HD] = dk
                acc[span, HD:] = dv
    for store in stores:
        store.wait()


def backward(rows, pack, d_attn_t, attn_t, stats, after):
    return pl.pallas_call(
        backward_kernel,
        out_shape=[shape((TOK, HQ * HD)), shape((TOK, 2 * HD)), TOKEN],
        in_specs=[VMEM] * 5 + [ANY],
        out_specs=[ANY, VMEM, VMEM],
        scratch_shapes=[
            pltpu.VMEM((HD, TOK), BF16),
            pltpu.VMEM((TOK, PAIR * TOK), BF16),
            pltpu.VMEM((TOK, PAIR * TOK), BF16),
            pltpu.VMEM((TOK, 2 * HD), F32),
            pltpu.VMEM((HQ, TOK, HD), BF16),
            pltpu.SemaphoreType.DMA((HQ,)),
        ],
        compiler_params=params(24),
        name="backward",
        cost_estimate=cost(30 * 10**9, 8 * 2**20, HQ * 655360),
    )(rows, pack, d_attn_t, attn_t, stats, after)


def add_pair_kernel(x_ref, keep_ref, got_hbm, *outs):
    *outs, token, got_ref, sems = outs
    for k in range(N_FSDP):
        pltpu.make_async_copy(got_hbm.at[k], got_ref.at[k], sems.at[k]).start()
    token[...] = jnp.zeros(token.shape, F32)
    x = x_ref[0]
    for k, out in enumerate(outs):
        shard = lax.rem(x + k, N_FSDP)
        pltpu.make_async_copy(got_hbm.at[shard], got_ref.at[shard], sems.at[shard]).wait()
        out[...] = (keep_ref[shard].astype(F32) + got_ref[shard].astype(F32)).astype(out.dtype)


def add_pair(x, keep, got):
    rows = keep.shape[0] // N_FSDP
    dims = (rows, HALF)
    return pl.pallas_call(
        add_pair_kernel,
        out_shape=[shape(dims, F32)] + [shape(dims)] * 3 + [TOKEN],
        in_specs=[SMEM, VMEM, ANY],
        out_specs=[VMEM] * 5,
        scratch_shapes=[pltpu.VMEM((N_FSDP, *dims), BF16), pltpu.SemaphoreType.DMA((N_FSDP,))],
        compiler_params=params(4),
        name="add_pair",
        cost_estimate=cost(4 * rows * HALF, 10 * rows * HALF * 2),
    )(x, keep.reshape(N_FSDP, *dims), got.reshape(N_FSDP, *dims))


def sum4(parts):
    own, next_one, last, opposite = (part.astype(F32) for part in parts)
    return (own + opposite) + (next_one + last)


def split_z_kernel(z_ref, _, *refs):
    parts, outs, total = refs[:4], refs[4:8], refs[8]
    total[...] = sum4([r[...] for r in parts])
    size = SHARD // 4
    z = z_ref[0]
    for k, out in enumerate(outs):
        at = pl.multiple_of(lax.rem(z + k, 4) * size, size)
        out[...] = total[pl.ds(at, size), :].astype(out.dtype)


def split_z(z, after, parts):
    dims = (SHARD // 4, HALF)
    return pl.pallas_call(
        split_z_kernel,
        out_shape=[shape(dims, F32)] + [shape(dims)] * 3,
        in_specs=[SMEM, ANY] + [VMEM] * 4,
        out_specs=[VMEM] * 4,
        scratch_shapes=[pltpu.VMEM((SHARD, HALF), F32)],
        compiler_params=params(4),
        name="split_z",
        cost_estimate=cost(4 * SHARD * HALF, 10 * SHARD * HALF),
    )(z, after, *parts)


def sum4_kernel(factor, *refs):
    refs[4][...] = (sum4([r[...] for r in refs[:4]]) * factor).astype(BF16)


def sum_four(parts, factor=1.0):
    return pl.pallas_call(
        functools.partial(sum4_kernel, factor),
        out_shape=shape(parts[0].shape),
        in_specs=[VMEM] * 4,
        out_specs=VMEM,
        compiler_params=params(8),
        name="sum_four",
        cost_estimate=cost(4 * parts[0].size, 10 * parts[0].size),
    )(*parts)


def join_z_kernel(z_ref, *refs):
    parts, out = refs[:4], refs[4]
    size = SHARD // 4
    for k, ref in enumerate(parts):
        at = pl.multiple_of(lax.rem(z_ref[0] - k + 4, 4) * size, size)
        out[pl.ds(at, size), :] = ref[...]


def join_z(z, parts):
    return pl.pallas_call(
        join_z_kernel,
        out_shape=shape((SHARD, HALF)),
        in_specs=[SMEM] + [VMEM] * 4,
        out_specs=VMEM,
        compiler_params=params(4),
        name="join_z",
        cost_estimate=cost(0, 4 * SHARD * HALF),
    )(z, *parts)


def lay_out_kernel(core_ref, own, got, out):
    for part, side in ((own, core_ref[0]), (got, 1 - core_ref[0])):
        columns = pl.ds(pl.multiple_of(side * HALF, HALF), HALF)
        out[:, columns] = part[...].astype(F32)


def lay_out(core, own, got):
    return pl.pallas_call(
        lay_out_kernel,
        out_shape=shape((SHARD, D), F32),
        in_specs=[SMEM, VMEM, VMEM],
        out_specs=VMEM,
        compiler_params=params(4),
        name="lay_out",
        cost_estimate=cost(SHARD * D, 6 * SHARD * D),
    )(core, own, got)


def dp_shift(dy, dz, dc):
    pairs = []
    for i in range(32):
        y, z, c = i // 8, (i // 2) % 4, i % 2
        pairs.append((i, ((y + dy) % 4) * 8 + ((z + dz) % 4) * 2 + (c + dc) % 2))
    return pairs


def x_shift(k):
    return [(i, (i + k) % N_FSDP) for i in range(N_FSDP)]


def per_device(stash, stash_place, pack_start, d_out, out_weight):
    group = lax.axis_index("dp")
    x = lax.axis_index("fsdp")
    core = lax.rem(group, 2)
    z = lax.rem(group // 2, 4)
    held = stash.reshape(NB, BLK, WIDTH)
    peers = jnp.arange(NB, dtype=jnp.int32)
    holder = lax.shift_right_logical(stash_place, 5)
    slot = stash_place - holder * NB
    chosen = jnp.sum(jnp.where((holder == group) & (peers[:, None] != group), slot, 0), axis=1)
    x1, z1, core1 = x.reshape(1), z.reshape(1), core.reshape(1)

    incoming = lax.all_to_all(held.at[chosen].get(mode="promise_in_bounds"), "dp", split_axis=0, concat_axis=0, tiled=True)
    swap = dp_shift(0, 0, 1)
    half = lax.dynamic_slice_in_dim(out_weight, core * HALF, HALF, 1)
    weight_mine = [lax.ppermute(half, "fsdp", x_shift(k)) for k in (1, 2, 3)]
    weight_other = [lax.ppermute(part, "dp", swap) for part in weight_mine]
    d_attn_t = d_attn_transposed(x1, core1, out_weight, weight_mine, weight_other, d_out)

    pack = pack_start.reshape(1, TOK)
    rows, attn_t, stats, send = forward(group.reshape(1), stash_place, held, incoming, pack, d_out, d_attn_t)
    keep = keep_half(core1, attn_t, d_out)
    *parts, x_token = add_pair(x1, keep, lax.ppermute(send, "dp", swap))
    by_x = [parts[0]] + [lax.ppermute(parts[k], "fsdp", x_shift(k)) for k in (2, 1, 3)]
    grad_query, grad_keyval, token = backward(rows, pack, d_attn_t, attn_t, stats, x_token)
    by_z = split_z(z1, token, by_x)
    by_z = [by_z[0]] + [lax.ppermute(by_z[k], "dp", dp_shift(0, k, 0)) for k in (2, 1, 3)]
    z_sum = sum_four(by_z)
    by_y = [z_sum] + [lax.ppermute(z_sum, "dp", dp_shift(k, 0, 0)) for k in (1, 3, 2)]
    factor = (TOK * lax.axis_size("dp") * lax.axis_size("fsdp")) ** (-0.5)
    total = sum_four(by_y, factor)
    by_z = {k: lax.ppermute(total, "dp", dp_shift(0, k, 0)) for k in (1, 3, 2)}
    own = join_z(z1, [total] + [by_z[k] for k in (1, 2, 3)])
    grad_weight = lay_out(core1, own, lax.ppermute(own, "dp", swap))
    return (grad_query, grad_keyval, grad_weight)


def solution(mesh):
    in_specs = (
        P("dp", "fsdp", None, None, None),
        P(),
        P(("dp", "fsdp")),
        P(("dp", "fsdp"), None),
        P("fsdp", None),
    )
    out_specs = (P(("dp", "fsdp"), None), P(("dp", "fsdp"), None), P("fsdp", None))
    return jax.shard_map(
        per_device, mesh=mesh, in_specs=in_specs, out_specs=out_specs, check_vma=False
    )
```
